32 devices in a mesh: dp: 8 (over y, x, core), mp: 4 (over z).
Axes of the slice: x: 2, y: 2, z: 4, core: 2. Of those that a mesh axis runs over, the one named last changes fastest.
Arguments:
- features: bfloat16 [16384, 2, 512], P('dp'), may hold values from -27 to 27
- projection: bfloat16 [512, 256], replicated, may hold values from -1 to 1
- prototypes: float32 [3000, 256], P('mp'), may hold values from -7 to 7
Outputs:
- grad_prototypes: float32 [3000, 256], P('mp')
- grad_projection: float32 [512, 256], replicated
- loss: float32 [], replicated
The draws below stay inside these ranges and needn't reach their ends.
All inputs are finite; a program needn't handle non-finite values.
Results may differ from the reference program's by a relative error of at most 0.0019.
The reference program's roundings to bfloat16 on the way count: a program that leaves them out, or rounds other values in their place, can miss the bound.
Values may be sent and summed in bfloat16 or wider, within the bound.
No kernel may reach another device: no remote copies, remote signals or barrier semaphores. Data moves between devices by JAX's collectives and lax.ppermute only.
A program may use at most 128 MiB of HBM per device.

```python
import math
import jax
import jax.numpy as jnp
from jax import lax

B_DEV = 2048
E = 512
P_SIZE = 256
K = 3000
ITERS = 3
WINDOW_BATCH = 16384


def shared_common(key):
    return jnp.clip(jax.random.normal(jax.random.fold_in(key, 101), (E,), jnp.float32), -3.0, 3.0)


def shared_direction(key):
    signs = jax.random.randint(jax.random.fold_in(key, 202), (P_SIZE,), 0, 2)
    return (2 * signs - 1).astype(jnp.float32) * (1.0 / math.sqrt(P_SIZE))


def draw_features(key, part):
    noise_key, scale_key, step_key, pick_key = jax.random.split(jax.random.fold_in(key, 303), 4)
    block_count = WINDOW_BATCH // B_DEV
    common = shared_common(key)[None, None, :]
    spread = jnp.exp(jax.random.uniform(scale_key, (block_count,), jnp.float32, math.log(1.0 / 3.0), 0.0))
    picked = jax.random.randint(pick_key, (), 0, block_count)
    block_scale = jnp.where(jnp.arange(block_count) == picked, 0.05, spread)
    scale_rows = jnp.repeat(block_scale, B_DEV, total_repeat_length=WINDOW_BATCH)[:, None, None]
    block_level = jax.random.uniform(step_key, (block_count,), jnp.float32, 0.0, 3.0)
    level_rows = jnp.repeat(block_level, B_DEV, total_repeat_length=WINDOW_BATCH)[:, None, None]
    noise_part = jnp.clip(jax.random.normal(noise_key, (WINDOW_BATCH, 2, E), jnp.float32), -6.0, 6.0)
    result = (noise_part + level_rows * common) * scale_rows
    return result.astype(jnp.bfloat16)


def draw_projection(key, part):
    noise = jnp.clip(jax.random.normal(jax.random.fold_in(key, 404), (E, P_SIZE), jnp.float32), -6.0, 6.0)
    common = shared_common(key)
    direction = shared_direction(key)
    result = noise * (1.0 / math.sqrt(E)) + common[:, None] * direction[None, :] * (math.sqrt(P_SIZE) / E)
    return result.astype(jnp.bfloat16)


def draw_prototypes(key, part):
    noise = jnp.clip(jax.random.normal(jax.random.fold_in(key, 505), (K, P_SIZE), jnp.float32), -6.0, 6.0)
    direction = shared_direction(key)
    rise = 0.4 * jnp.arange(K, dtype=jnp.float32) / (K - 1)
    result = noise + rise[:, None] * math.sqrt(P_SIZE) * direction[None, :]
    return result.astype(jnp.float32)


def setup_inputs(seed: int = 0) -> dict:
    key_of = jax.random.split(jax.random.key(seed), 4)
    features = draw_features(jax.random.fold_in(key_of[3], 71), 0)
    projection = draw_projection(jax.random.fold_in(key_of[3], 71), 0)
    prototypes = draw_prototypes(jax.random.fold_in(key_of[3], 71), 0)
    return dict(features=features, projection=projection, prototypes=prototypes)


EPSILON_CODES = 0.05
SOFTMAX_TEMPER = 0.1
LOSS_FACTOR = 4096.0
TINY = 1e-06
HIGH = lax.Precision.HIGHEST

def unit_rows(values):
    inverse = lax.rsqrt(lax.optimization_barrier(jnp.sum(values * values, axis=-1, keepdims=True)) + TINY)
    return (values * inverse, inverse)

def embed_block(block_feats, projection):
    raw_embed = jnp.einsum('bve,ep->bvp', block_feats.astype(jnp.float32), projection.astype(jnp.float32), precision=HIGH)
    return unit_rows(raw_embed)

def reference(features, projection, prototypes):
    proto_unit, proto_inverse = unit_rows(prototypes)
    proto_half = proto_unit.astype(jnp.bfloat16)
    proto_wide = proto_half.astype(jnp.float32)
    embed_all, unused_inverse = embed_block(features, projection)
    embed_all = embed_all.astype(jnp.bfloat16).astype(jnp.float32)
    prototype_logits = jnp.einsum('bvp,kp->bvk', embed_all, proto_wide, precision=HIGH)
    col_scale = jnp.ones((2, K), jnp.float32)
    row_scale = jnp.ones((WINDOW_BATCH, 2), jnp.float32)
    for iteration in range(ITERS):
        col_scale = 1.0 / jnp.einsum('bvk,bv->vk', jnp.exp(prototype_logits * (1.0 / EPSILON_CODES)), row_scale, precision=HIGH)
        row_scale = 1.0 / jnp.einsum('bvk,vk->bv', jnp.exp(prototype_logits * (1.0 / EPSILON_CODES)), col_scale, precision=HIGH)
    block_rows = math.gcd(WINDOW_BATCH, 4096)
    gradient_factor = LOSS_FACTOR / (2.0 * WINDOW_BATCH * SOFTMAX_TEMPER)

    def block_terms(totals, block_index):
        proto_acc, weight_acc, loss_running_sum = totals
        row_start = (block_index * block_rows).astype(jnp.int32)
        block_feats = lax.dynamic_slice_in_dim(features, row_start, block_rows, 0)
        embed_unit, embed_inverse = embed_block(block_feats, projection)
        embed_wide = embed_unit.astype(jnp.bfloat16).astype(jnp.float32)
        block_logits = lax.dynamic_slice_in_dim(prototype_logits, row_start, block_rows, 0)
        block_rowsc = lax.dynamic_slice_in_dim(row_scale, row_start, block_rows, 0)
        assignments = jnp.exp(block_logits * (1.0 / EPSILON_CODES)) * col_scale[None] * block_rowsc[..., None]
        softmax_exponent = jnp.exp(block_logits * (1.0 / SOFTMAX_TEMPER))
        softmax_denominator = lax.optimization_barrier(jnp.sum(softmax_exponent, axis=-1))
        swapped_targets = assignments[:, ::-1]
        grad_half = ((softmax_exponent / softmax_denominator[..., None] - swapped_targets) * gradient_factor).astype(jnp.bfloat16)
        grad_wide = grad_half.astype(jnp.float32)
        loss_running_sum = loss_running_sum + jnp.sum(swapped_targets * (block_logits * (1.0 / SOFTMAX_TEMPER) - jnp.log(softmax_denominator)[..., None]))
        proto_acc = proto_acc + jnp.einsum('bvk,bvp->kp', grad_wide, embed_wide, precision=HIGH)
        grad_unit = jnp.einsum('bvk,kp->bvp', grad_wide, proto_wide, precision=HIGH)
        along_unit = lax.optimization_barrier(jnp.sum(embed_unit * grad_unit, axis=-1, keepdims=True))
        grad_raw = ((grad_unit - embed_unit * along_unit) * embed_inverse).astype(jnp.bfloat16)
        weight_acc = weight_acc + jnp.einsum('bve,bvp->ep', block_feats.astype(jnp.float32), grad_raw.astype(jnp.float32), precision=HIGH)
        return ((proto_acc, weight_acc, loss_running_sum), None)
    initial = (jnp.zeros((K, P_SIZE), jnp.float32), jnp.zeros((E, P_SIZE), jnp.float32), jnp.zeros((), jnp.float32))
    totals, unused_out = lax.scan(block_terms, initial, jnp.arange(WINDOW_BATCH // block_rows, dtype=jnp.int32))
    proto_grad, weight_grad, loss_total = totals
    along_proto = lax.optimization_barrier(jnp.sum(proto_unit * proto_grad, axis=-1, keepdims=True))
    grad_protos = (proto_grad - proto_unit * along_proto) * proto_inverse
    loss_value = -loss_total / (2.0 * WINDOW_BATCH)
    return (grad_protos, weight_grad, loss_value)
```

```python
import functools

import jax
import jax.numpy as jnp
from jax import lax
from jax.experimental import pallas as pl
from jax.experimental.pallas import tpu as pltpu
from jax.sharding import PartitionSpec as P

ITERS = 3
EPSILON_CODES = 0.05
SOFTMAX_TEMPER = 0.1
LOSS_FACTOR = 4096.0
TINY = 1e-06
LANES = 128
VMEM_LIMIT = 48 * 1024 * 1024


def swap(values, axis, size, offset):
    return lax.ppermute(values, axis, [(i, i ^ offset) for i in range(size)])


def stages(size, first):
    bits = size.bit_length() - 1
    groups, done = [], 0
    while done < bits:
        width = min(first if not groups else 2, bits - done)
        groups.append((done, width))
        done += width
    return groups


def sum_over(values, axis, first):
    size = lax.axis_size(axis)
    for low, width in stages(size, first):
        parts = [swap(values, axis, size, k << low) for k in range(1, 1 << width)]
        values = functools.reduce(jnp.add, parts, values)
    return values


def scatter_sum(values, axis, first):
    size = lax.axis_size(axis)
    me = lax.axis_index(axis)
    block = values.shape[1:]
    values = values[None]
    for low, width in stages(size, first):
        ways = 1 << width
        rest = values.shape[1] // ways
        values = values.reshape((rest, ways) + block)
        mine = (me >> low) & (ways - 1)
        own = lax.dynamic_index_in_dim(values, mine, 1, keepdims=False)
        for k in range(1, ways):
            out = lax.dynamic_index_in_dim(values, mine ^ k, 1, keepdims=False)
            own = own + swap(out, axis, size, k << low)
        values = own[None]
    return values.reshape(block)


def gather_blocks(values, axis, first):
    size = lax.axis_size(axis)
    me = lax.axis_index(axis)
    block = values.shape
    values = values[None]
    for low, width in reversed(stages(size, first)):
        ways = 1 << width
        mine = (me >> low) & (ways - 1)
        parts = [values] + [swap(values, axis, size, k << low) for k in range(1, ways)]
        out = jnp.zeros((values.shape[0], ways) + block, values.dtype)
        for k, part in enumerate(parts):
            out = lax.dynamic_update_slice_in_dim(out, part[:, None], mine ^ k, 1)
        values = out.reshape((-1,) + block)
    return values


def gather_over(values, axis):
    size = lax.axis_size(axis)
    me = lax.axis_index(axis)
    parts = [values] + [swap(values, axis, size, k) for k in range(1, size)]
    out = jnp.zeros((size,) + values.shape, values.dtype)
    for k, part in enumerate(parts):
        out = lax.dynamic_update_slice_in_dim(out, part[None], me ^ k, 0)
    return out


def logits_of(proto_ref, rows):
    return lax.dot_general(
        proto_ref[...], rows, (((1,), (1,)), ((), ())), preferred_element_type=jnp.float32
    )


def lane_sums(values):
    total = values[:, :LANES]
    for start in range(LANES, values.shape[1], LANES):
        total = total + values[:, start : start + LANES]
    return total


def as_column(row):
    return jnp.transpose(jnp.broadcast_to(row, (LANES, row.shape[1])))


def widen(column, width):
    return jnp.concatenate([column] * (width // LANES), axis=1)


def first_kernel(valid, proto_ref, rows_ref, col_ref, soft_ref, acc_ref):
    view, tile = pl.program_id(0), pl.program_id(1)
    logits = logits_of(proto_ref, rows_ref[0])
    soft = jnp.exp(logits * (1.0 / SOFTMAX_TEMPER))
    keep = lax.broadcasted_iota(jnp.int32, soft.shape, 0) < valid
    soft_ref[...] = jnp.sum(jnp.where(keep, soft, 0.0), axis=0)[None, None]
    part = lane_sums(soft * soft)

    @pl.when(tile == 0)
    def _():
        acc_ref[...] = part

    @pl.when(tile > 0)
    def _():
        acc_ref[...] += part

    @pl.when(tile == pl.num_programs(1) - 1)
    def _():
        col_ref[...] = jnp.sum(jnp.transpose(acc_ref[...]), axis=0)[None, None]


def col_kernel(proto_ref, rows_ref, sums_ref, col_ref, acc_ref):
    view, tile = pl.program_id(0), pl.program_id(1)
    logits = logits_of(proto_ref, rows_ref[0])
    transport = jnp.exp(logits * (1.0 / EPSILON_CODES))
    part = lane_sums(transport * (1.0 / sums_ref[0]))

    @pl.when(tile == 0)
    def _():
        acc_ref[...] = part

    @pl.when(tile > 0)
    def _():
        acc_ref[...] += part

    @pl.when(tile == pl.num_programs(1) - 1)
    def _():
        col_ref[...] = jnp.sum(jnp.transpose(acc_ref[...]), axis=0)[None, None]


def row_kernel(valid, proto_ref, rows_ref, sums_ref, row_ref, scale_ref):
    tile = pl.program_id(1)

    @pl.when(tile == 0)
    def _():
        sums = sums_ref[0]
        keep = lax.broadcasted_iota(jnp.int32, sums.shape, 1) < valid
        scale_ref[...] = as_column(jnp.where(keep, 1.0 / sums, 0.0))

    logits = logits_of(proto_ref, rows_ref[0])
    transport = jnp.exp(logits * (1.0 / EPSILON_CODES))
    scaled = transport * widen(scale_ref[...], transport.shape[1])
    row_ref[...] = jnp.sum(scaled, axis=0)[None, None]


def grad_of(factor, proto_ref, rows_ref, denoms_ref, sums_ref, scale_ref):
    soft, target, logits = [], [], []
    for view in range(2):
        scores = logits_of(proto_ref, rows_ref[view])
        value = jnp.exp(scores * (1.0 / SOFTMAX_TEMPER))
        scaled = value * value * widen(scale_ref[view], scores.shape[1])
        soft.append(value * (factor / denoms_ref[view]))
        target.append(scaled * (1.0 / sums_ref[view]))
        logits.append(scores)
    grads, loss = [], 0.0
    for view in range(2):
        swapped = target[1 - view]
        grads.append((soft[view] - swapped * factor).astype(jnp.bfloat16))
        terms = logits[view] * (1.0 / SOFTMAX_TEMPER) - jnp.log(denoms_ref[view])
        loss = loss + jnp.sum(swapped * terms, axis=0, keepdims=True)
    return grads, loss


def set_scales(valid, block, cols_ref, scale_ref):
    @pl.when(pl.program_id(0) == 0)
    def _():
        for view in range(2):
            sums = cols_ref[view]
            place = lax.broadcasted_iota(jnp.int32, sums.shape, 1)
            keep = lax.rem(place, block) < valid
            scale_ref[view] = as_column(jnp.where(keep, 1.0 / sums, 0.0))


def proto_grad_kernel(
    valid, block, factor, proto_ref, rows_ref, denoms_ref, sums_ref, cols_ref, out_ref, loss_ref, scale_ref
):
    set_scales(valid, block, cols_ref, scale_ref)
    grads, loss = grad_of(factor, proto_ref, rows_ref, denoms_ref, sums_ref, scale_ref)
    part = sum(
        lax.dot_general(
            grads[view], rows_ref[view], (((1,), (0,)), ((), ())), preferred_element_type=jnp.float32
        )
        for view in range(2)
    )
    loss_ref[...] = loss

    @pl.when(pl.program_id(0) == 0)
    def _():
        out_ref[...] = part

    @pl.when(pl.program_id(0) > 0)
    def _():
        out_ref[...] += part


def embed_grad_kernel(
    valid, block, factor, proto_ref, rows_ref, denoms_ref, sums_ref, cols_ref, out_ref, scale_ref
):
    set_scales(valid, block, cols_ref, scale_ref)
    grads, _ = grad_of(factor, proto_ref, rows_ref, denoms_ref, sums_ref, scale_ref)
    for view in range(2):
        out_ref[view] = lax.dot_general(
            grads[view], proto_ref[...], (((0,), (0,)), ((), ())), preferred_element_type=jnp.float32
        )


def whole(shape):
    return pl.BlockSpec(shape, lambda *_: (0,) * len(shape))


def params(grid):
    return pltpu.CompilerParams(
        dimension_semantics=("arbitrary",) * grid, vmem_limit_bytes=VMEM_LIMIT
    )


def cost(protos, rows, products):
    return pl.CostEstimate(
        flops=2 * protos * rows * 256 * products, bytes_accessed=2 * 256 * (protos + rows),
        transcendentals=protos * rows,
    )


def sinkhorn_calls(valid, proto_half, embed_half):
    protos, width = proto_half.shape
    views, rows, _ = embed_half.shape
    tile = min(512, rows)
    grid = (views, rows // tile)
    proto_spec = whole((protos, width))
    rows_spec = pl.BlockSpec((1, tile, width), lambda v, t: (v, t, 0))
    row_spec = pl.BlockSpec((1, 1, tile), lambda v, t: (v, 0, t))
    col_spec = pl.BlockSpec((1, 1, protos), lambda v, t: (v, 0, 0))
    row_shape = jax.ShapeDtypeStruct((views, 1, rows), jnp.float32)
    col_shape = jax.ShapeDtypeStruct((views, 1, protos), jnp.float32)
    column = pltpu.VMEM((protos, LANES), jnp.float32)
    common = dict(grid=grid, compiler_params=params(2), cost_estimate=cost(protos, 2 * rows, 1))
    first = pl.pallas_call(
        functools.partial(first_kernel, valid), in_specs=[proto_spec, rows_spec],
        out_specs=[col_spec, row_spec], out_shape=[col_shape, row_shape],
        scratch_shapes=[column], name="first_totals", **common,
    )
    col = pl.pallas_call(
        col_kernel, in_specs=[proto_spec, rows_spec, row_spec], out_specs=col_spec,
        out_shape=col_shape, scratch_shapes=[column], name="column_totals", **common,
    )
    row = pl.pallas_call(
        functools.partial(row_kernel, valid), in_specs=[proto_spec, rows_spec, col_spec],
        out_specs=row_spec, out_shape=row_shape, scratch_shapes=[column], name="row_totals", **common,
    )
    return (
        lambda: first(proto_half, embed_half),
        lambda sums: col(proto_half, embed_half, sums),
        lambda sums: row(proto_half, embed_half, sums),
    )


def grad_call(kernel, tile, loss, proto_half, embed_half, denoms, row_sums, col_sums, **names):
    protos, width = proto_half.shape
    views, rows, _ = embed_half.shape
    tile = min(tile, rows)
    row_spec = pl.BlockSpec((views, 1, tile), lambda t: (0, 0, t))
    rows_spec = pl.BlockSpec((views, tile, width), lambda t: (0, t, 0))
    if loss:
        out_specs = [whole((protos, width)), pl.BlockSpec((1, tile), lambda t: (0, t))]
        out_shape = [
            jax.ShapeDtypeStruct((protos, width), jnp.float32),
            jax.ShapeDtypeStruct((1, rows), jnp.float32),
        ]
    else:
        out_specs = rows_spec
        out_shape = jax.ShapeDtypeStruct((views, rows, width), jnp.float32)
    return pl.pallas_call(
        kernel, grid=(rows // tile,),
        in_specs=[
            whole((protos, width)), rows_spec, row_spec, row_spec, whole((views, 1, protos)),
        ],
        out_specs=out_specs, out_shape=out_shape,
        scratch_shapes=[pltpu.VMEM((views, protos, LANES), jnp.float32)],
        compiler_params=params(1), cost_estimate=cost(protos, 2 * rows, 2), **names,
    )(proto_half, embed_half, denoms, row_sums, col_sums)


def unit_rows(values):
    inverse = lax.rsqrt(jnp.sum(values * values, axis=-1, keepdims=True) + TINY)
    return (values * inverse, inverse)


def body(features, projection, prototypes):
    local_rows = features.shape[0]
    shards = lax.axis_size("dp")
    own_count = local_rows // lax.axis_size("mp")
    batch_row_count = local_rows * shards
    factor = LOSS_FACTOR / (2.0 * batch_row_count * SOFTMAX_TEMPER)
    valid, width = prototypes.shape
    block = -(-valid // LANES) * LANES
    first_row = lax.axis_index("mp") * own_count

    proto_unit, proto_inverse = unit_rows(prototypes)
    proto_half = jnp.pad(proto_unit.astype(jnp.bfloat16), ((0, block - valid), (0, 0)))
    all_proto = lax.all_gather(proto_half, "mp", axis=0, tiled=True)

    raw_embed = jnp.einsum("bve,ep->vbp", features, projection, preferred_element_type=jnp.float32)
    embed_unit, embed_inverse = unit_rows(raw_embed)
    embed_half = embed_unit.astype(jnp.bfloat16)

    first, col, row = sinkhorn_calls(valid, proto_half, embed_half)
    col_part, soft_part = first()
    col_sums = sum_over(col_part, "dp", 1)
    both = sum_over(jnp.concatenate([row(col_sums), soft_part]), "mp", 2)
    row_sums, denoms = both[:2], both[2:]
    for iteration in range(1, ITERS):
        col_sums = sum_over(col(row_sums), "dp", 1)
        row_sums = sum_over(row(col_sums), "mp", 2)

    own = functools.partial(lax.dynamic_slice_in_dim, start_index=first_row, slice_size=own_count)
    all_cols = gather_over(col_sums, "mp")
    all_cols = jnp.transpose(all_cols, (1, 2, 0, 3)).reshape(2, 1, -1)
    grad_unit = grad_call(
        functools.partial(embed_grad_kernel, valid, block, factor), 128, False,
        all_proto, own(embed_half, axis=1), own(denoms, axis=2), own(row_sums, axis=2), all_cols,
        name="embed_gradient",
    )
    own_unit, own_inverse = own(embed_unit, axis=1), own(embed_inverse, axis=1)
    along_unit = jnp.sum(own_unit * grad_unit, axis=-1, keepdims=True)
    grad_raw = ((grad_unit - own_unit * along_unit) * own_inverse).astype(jnp.bfloat16)
    weight_part = jnp.einsum(
        "bve,vbp->ep", own(features, axis=0), grad_raw, preferred_element_type=jnp.float32
    )

    proto_part, loss_rows = grad_call(
        functools.partial(proto_grad_kernel, valid, block, factor), 256, True,
        proto_half, embed_half, denoms, row_sums, col_sums, name="proto_gradient",
    )
    loss_row = jnp.broadcast_to(jnp.sum(loss_rows), (shards, 8, width))

    weight_part = jnp.concatenate([weight_part.reshape(shards, -1, width), loss_row], axis=1)
    weight_sum = sum_over(scatter_sum(weight_part, "dp", 1), "mp", 2)
    loss_value = -weight_sum[-1, 0] / (2.0 * batch_row_count)
    weight_grad = gather_blocks(weight_sum[:-8], "dp", 1).reshape(projection.shape)

    proto_sum = scatter_sum(proto_part.reshape(shards, -1, width), "dp", 1)
    proto_grad = gather_blocks(proto_sum, "dp", 1).reshape(block, width)[:valid]
    along_proto = jnp.sum(proto_unit * proto_grad, axis=-1, keepdims=True)
    grad_protos = (proto_grad - proto_unit * along_proto) * proto_inverse
    return (grad_protos, weight_grad, loss_value)


def solution(mesh):
    return jax.shard_map(
        body,
        mesh=mesh,
        in_specs=(P("dp", None, None), P(), P("mp", None)),
        out_specs=(P("mp", None), P(), P()),
        check_vma=False,
    )
```

```python
import functools

import jax
import jax.numpy as jnp
from jax import lax
from jax.experimental import pallas as pl
from jax.experimental.pallas import tpu as pltpu
from jax.sharding import PartitionSpec as P

ITERS = 3
EPSILON_CODES = 0.05
SOFTMAX_TEMPER = 0.1
LOSS_FACTOR = 4096.0
TINY = 1e-06
LOG2_E = 1.4426950408889634
LANES = 128
CHUNK = 256
VMEM_LIMIT = 20 * 1024 * 1024


def swap(values, axis, size, offset):
    return lax.ppermute(values, axis, [(i, i ^ offset) for i in range(size)])


def stages(size, first):
    bits = size.bit_length() - 1
    groups, done = [], 0
    while done < bits:
        width = min(first if not groups else 2, bits - done)
        groups.append((done, width))
        done += width
    return groups


def sum_over(values, axis, first):
    size = lax.axis_size(axis)
    for low, width in stages(size, first):
        parts = [swap(values, axis, size, k << low) for k in range(1, 1 << width)]
        values = functools.reduce(jnp.add, parts, values)
    return values


def scatter_sum(values, axis, first):
    size = lax.axis_size(axis)
    me = lax.axis_index(axis)
    block = values.shape[1:]
    values = values[None]
    for low, width in stages(size, first):
        ways = 1 << width
        rest = values.shape[1] // ways
        values = values.reshape((rest, ways) + block)
        mine = (me >> low) & (ways - 1)
        own = lax.dynamic_index_in_dim(values, mine, 1, keepdims=False)
        for k in range(1, ways):
            out = lax.dynamic_index_in_dim(values, mine ^ k, 1, keepdims=False)
            own = own + swap(out, axis, size, k << low)
        values = own[None]
    return values.reshape(block)


def gather_blocks(values, axis, first):
    size = lax.axis_size(axis)
    me = lax.axis_index(axis)
    block = values.shape
    values = values[None]
    for low, width in reversed(stages(size, first)):
        ways = 1 << width
        mine = (me >> low) & (ways - 1)
        parts = [values] + [swap(values, axis, size, k << low) for k in range(1, ways)]
        out = jnp.zeros((values.shape[0], ways) + block, values.dtype)
        for k, part in enumerate(parts):
            out = lax.dynamic_update_slice_in_dim(out, part[:, None], mine ^ k, 1)
        values = out.reshape((-1,) + block)
    return values


NN = (((1,), (0,)), ((), ()))
NT = (((1,), (1,)), ((), ()))


def product(left, right, dims):
    return lax.dot_general(left, right, dims, preferred_element_type=jnp.float32)


def lane_sums(values):
    total = values[:, :LANES]
    for start in range(LANES, values.shape[1], LANES):
        total = total + values[:, start : start + LANES]
    return total


def as_row(column):
    return jnp.sum(jnp.transpose(column), axis=0, keepdims=True)


def as_column(row):
    return jnp.transpose(jnp.broadcast_to(row, (LANES, row.shape[1])))


def widen(column, width):
    return jnp.concatenate([column] * (width // LANES), axis=1)


def column_scale(valid, sums):
    keep = lax.broadcasted_iota(jnp.int32, sums.shape, 1) < valid
    return as_column(jnp.where(keep, 1.0 / sums, 0.0))


def tiles(ref, width, step):
    count = ref.shape[-1] // width

    def one(index, _):
        step(index // count, pl.ds(pl.multiple_of(lax.rem(index, count) * width, width), width))
        return 0

    lax.fori_loop(0, 2 * count, one, 0)


def first_kernel(
    valid, width, feats_ref, proj_ref, proto_ref, soft_ref, raw_ref, half_ref, col_ref, denom_ref, acc_ref
):
    acc_ref[...] = jnp.zeros_like(acc_ref)
    edge = valid // 8 * 8

    def step(view, lanes):
        raw = product(proj_ref[...], feats_ref[view, lanes, :], NT)
        raw_ref[view, :, lanes] = raw
        inverse = lax.rsqrt(jnp.sum(raw * raw, axis=0, keepdims=True) + TINY)
        half = (raw * inverse).astype(jnp.bfloat16)
        half_ref[view, :, lanes] = half
        denom = jnp.zeros((8, width), jnp.float32)
        for start in range(0, proto_ref.shape[0], CHUNK):
            logits = product(proto_ref[start : start + CHUNK], half, NN)
            soft = jnp.exp2(logits * (LOG2_E / SOFTMAX_TEMPER))
            if start + CHUNK > edge:
                place = lax.broadcasted_iota(jnp.int32, soft.shape, 0) + start
                soft = jnp.where(place < valid, soft, 0.0)
            soft_ref[view, start : start + CHUNK, lanes] = soft
            denom = denom + jnp.sum(soft.reshape(-1, 8, width), axis=0)
            acc_ref[view, start : start + CHUNK] += lane_sums(soft * soft)
        denom_ref[view, :, lanes] = jnp.sum(denom, axis=0, keepdims=True)

    tiles(denom_ref, width, step)
    for view in range(2):
        col_ref[view] = as_row(acc_ref[view])


def row_kernel(valid, width, soft_ref, sums_ref, row_ref, scale_ref):
    for view in range(2):
        scale_ref[view] = column_scale(valid, sums_ref[view])

    def step(view, lanes):
        total = jnp.zeros((8, width), jnp.float32)
        for start in range(0, soft_ref.shape[1], 8):
            soft = soft_ref[view, start : start + 8, lanes]
            total = total + soft * soft * widen(scale_ref[view, start : start + 8], width)
        row_ref[view, :, lanes] = jnp.sum(total, axis=0, keepdims=True)

    tiles(row_ref, width, step)


def col_kernel(width, soft_ref, sums_ref, col_ref, acc_ref):
    acc_ref[...] = jnp.zeros_like(acc_ref)

    def step(view, lanes):
        scale = jnp.broadcast_to(1.0 / sums_ref[view, :, lanes], (8, width))
        for start in range(0, soft_ref.shape[1], 8):
            soft = soft_ref[view, start : start + 8, lanes]
            acc_ref[view, start : start + 8] += lane_sums(soft * soft * scale)

    tiles(sums_ref, width, step)
    for view in range(2):
        col_ref[view] = as_row(acc_ref[view])


def grad_kernel(
    valid, width, factor, feats_ref, proto_ref, turned_ref, soft_ref, raw_ref, half_ref, denom_ref, row_ref,
    col_ref, proto_out, proj_out, loss_ref, scale_ref, grad_ref, turn_ref,
):
    for view in range(2):
        scale_ref[view] = column_scale(valid, col_ref[view])
    proto_out[...] = jnp.zeros_like(proto_out)
    turn_ref[...] = jnp.zeros_like(turn_ref)

    def step(index, loss):
        lanes = pl.ds(index * width, width)
        both = lambda ref: jnp.concatenate([ref[view, :, lanes] for view in range(2)], axis=1)
        rows, denoms = factor / both(row_ref), factor / both(denom_ref)
        halves = both(half_ref)
        for start in range(0, proto_ref.shape[0], CHUNK):
            part = slice(start, start + CHUNK)
            logits = product(proto_ref[part], halves, NN)
            softs = [soft_ref[view, part, lanes] for view in range(2)]
            for view in range(2):
                here, there = (slice(at * width, (at + 1) * width) for at in (view, 1 - view))
                target = softs[1 - view] * softs[1 - view] * widen(scale_ref[1 - view, part], width)
                target = target * rows[:, there]
                loss = loss + jnp.sum((logits[:, here] * target).reshape(-1, 8, width), axis=0)
                grad_ref[part, here] = (softs[view] * denoms[:, here] - target).astype(jnp.bfloat16)
        proto_out[...] += product(grad_ref[...], halves, NT)
        raw = both(raw_ref)
        inverse = lax.rsqrt(jnp.sum(raw * raw, axis=0, keepdims=True) + TINY)
        unit = raw * inverse
        grad_unit = product(turned_ref[...], grad_ref[...], NN)
        along = jnp.sum(unit * grad_unit, axis=0, keepdims=True)
        grad_raw = ((grad_unit - unit * along) * inverse).astype(jnp.bfloat16)
        feats = jnp.concatenate([feats_ref[view, lanes, :] for view in range(2)], axis=0)
        turn_ref[...] += product(grad_raw, feats, NN)
        return loss

    loss = jnp.zeros((8, width), jnp.float32)
    for index in range(row_ref.shape[-1] // width):
        loss = step(index, loss)
    proj_out[...] = jnp.transpose(turn_ref[...])
    logs = jnp.log(denom_ref[0]) + jnp.log(denom_ref[1])
    loss = jnp.sum(loss, axis=0, keepdims=True) * (1.0 / (SOFTMAX_TEMPER * factor))
    loss_ref[...] = jnp.broadcast_to(
        jnp.sum(loss, axis=1, keepdims=True) - jnp.sum(logs, axis=1, keepdims=True) * (1.0 / lax.axis_size("mp")),
        loss_ref.shape,
    )


IN_VMEM = pl.BlockSpec(memory_space=pltpu.VMEM)


def call(kernel, name, out_shapes, scratch, work, *args):
    outs = [jax.ShapeDtypeStruct(shape, dtype) for shape, dtype in out_shapes]
    return pl.pallas_call(
        kernel, in_specs=[IN_VMEM] * len(args), out_specs=[IN_VMEM] * len(outs), out_shape=outs,
        scratch_shapes=[pltpu.VMEM(shape, dtype) for shape, dtype in scratch],
        compiler_params=pltpu.CompilerParams(vmem_limit_bytes=VMEM_LIMIT),
        cost_estimate=pl.CostEstimate(flops=work, bytes_accessed=2**20, transcendentals=0), name=name,
    )(*args)


def unit_rows(values):
    inverse = lax.rsqrt(jnp.sum(values * values, axis=-1, keepdims=True) + TINY)
    return (values * inverse, inverse)


def body(features, projection, prototypes):
    rows = features.shape[0]
    shards = lax.axis_size("dp")
    batch_row_count = rows * shards
    factor = LOSS_FACTOR / (2.0 * batch_row_count * SOFTMAX_TEMPER)
    valid, width = prototypes.shape
    block = -(-valid // LANES) * LANES
    single, half_type = jnp.float32, jnp.bfloat16

    proto_unit, proto_inverse = unit_rows(prototypes)
    proto_half = jnp.pad(proto_unit.astype(half_type), ((0, block - valid), (0, 0)))
    feats = jnp.transpose(features, (1, 0, 2))

    row_shape, col_shape = ((2, 1, rows), single), ((2, 1, block), single)
    column = ((2, block, LANES), single)
    work = 4 * rows * block * width
    soft, raw, half, col_part, soft_part = call(
        functools.partial(first_kernel, valid, min(2048, rows)), "first_totals",
        [((2, block, rows), single), ((2, width, rows), single), ((2, width, rows), half_type), col_shape, row_shape],
        [column], work, feats, projection.T, proto_half,
    )
    row_call = functools.partial(
        call, functools.partial(row_kernel, valid, min(512, rows)), "row_totals", [row_shape], [column], work, soft
    )
    col_call = functools.partial(
        call, functools.partial(col_kernel, min(512, rows)), "column_totals", [col_shape], [column], work, soft
    )

    col_sums = sum_over(col_part, "dp", 1)
    both = sum_over(jnp.concatenate([row_call(col_sums)[0], soft_part]), "mp", 2)
    row_sums, denoms = both[:2], both[2:]
    for iteration in range(1, ITERS):
        col_sums = sum_over(col_call(row_sums)[0], "dp", 1)
        row_sums = sum_over(row_call(col_sums)[0], "mp", 2)

    grad_tile = min(512, rows)
    proto_part, proj_part, loss = call(
        functools.partial(grad_kernel, valid, grad_tile, factor), "gradients",
        [((block, width), single), (projection.shape, single), ((8, width), single)],
        [column, ((block, 2 * grad_tile), half_type), (projection.shape[::-1], single)],
        3 * work, feats, proto_half, proto_half.T, soft, raw, half, denoms, row_sums, col_sums,
    )
    loss_rows = jnp.broadcast_to(loss[None], (shards,) + loss.shape)
    proj_part = jnp.concatenate([proj_part.reshape(shards, -1, width), loss_rows], axis=1)
    proj_sum = sum_over(scatter_sum(proj_part, "dp", 1), "mp", 2)
    loss_value = -proj_sum[-1, 0] / (2.0 * batch_row_count)
    proj_grad = gather_blocks(proj_sum[:-8], "dp", 1).reshape(projection.shape)

    proto_sum = scatter_sum(proto_part.reshape(shards, -1, width), "dp", 1)
    proto_grad = gather_blocks(proto_sum, "dp", 1).reshape(block, width)[:valid]
    along_proto = jnp.sum(proto_unit * proto_grad, axis=-1, keepdims=True)
    grad_protos = (proto_grad - proto_unit * along_proto) * proto_inverse
    return (grad_protos, proj_grad, loss_value)


def solution(mesh):
    return jax.shard_map(
        body,
        mesh=mesh,
        in_specs=(P("dp", None, None), P(), P("mp", None)),
        out_specs=(P("mp", None), P(), P()),
        check_vma=False,
    )
```

```python
import functools

import jax
import jax.numpy as jnp
from jax import lax
from jax.experimental import pallas as pl
from jax.experimental.pallas import tpu as pltpu
from jax.sharding import PartitionSpec as P

ITERS = 3
EPSILON_CODES = 0.05
SOFTMAX_TEMPER = 0.1
LOSS_FACTOR = 4096.0
TINY = 1e-06
LOG2_E = 1.4426950408889634
LANES = 128
CHUNK = 256
VMEM_LIMIT = 20 * 1024 * 1024


def swap(values, axis, size, offset):
    return lax.ppermute(values, axis, [(i, i ^ offset) for i in range(size)])


def stages(size, first):
    bits = size.bit_length() - 1
    groups, done = [], 0
    while done < bits:
        width = min(first if not groups else 2, bits - done)
        groups.append((done, width))
        done += width
    return groups


def sum_over(values, axis, first):
    size = lax.axis_size(axis)
    for low, width in stages(size, first):
        parts = [swap(values, axis, size, k << low) for k in range(1, 1 << width)]
        values = functools.reduce(jnp.add, parts, values)
    return values


def scatter_sum(values, axis, first):
    size = lax.axis_size(axis)
    me = lax.axis_index(axis)
    block = values.shape[1:]
    values = values[None]
    for low, width in stages(size, first):
        ways = 1 << width
        rest = values.shape[1] // ways
        values = values.reshape((rest, ways) + block)
        mine = (me >> low) & (ways - 1)
        own = lax.dynamic_index_in_dim(values, mine, 1, keepdims=False)
        for k in range(1, ways):
            out = lax.dynamic_index_in_dim(values, mine ^ k, 1, keepdims=False)
            own = own + swap(out, axis, size, k << low)
        values = own[None]
    return values.reshape(block)


def gather_blocks(values, axis, first):
    size = lax.axis_size(axis)
    me = lax.axis_index(axis)
    block = values.shape
    values = values[None]
    for low, width in reversed(stages(size, first)):
        ways = 1 << width
        mine = (me >> low) & (ways - 1)
        parts = [values] + [swap(values, axis, size, k << low) for k in range(1, ways)]
        out = jnp.zeros((values.shape[0], ways) + block, values.dtype)
        for k, part in enumerate(parts):
            out = lax.dynamic_update_slice_in_dim(out, part[:, None], mine ^ k, 1)
        values = out.reshape((-1,) + block)
    return values


NN = (((1,), (0,)), ((), ()))
NT = (((1,), (1,)), ((), ()))


def product(left, right, dims):
    return lax.dot_general(left, right, dims, preferred_element_type=jnp.float32)


def unit_rows(values):
    inverse = lax.rsqrt(jnp.sum(values * values, axis=-1, keepdims=True) + TINY)
    return (values * inverse, inverse)


def unit_columns(values):
    inverse = lax.rsqrt(jnp.sum(values * values, axis=0, keepdims=True) + TINY)
    return (values * inverse, inverse)


def lane_sums(values):
    total = values[:, :LANES]
    for start in range(LANES, values.shape[1], LANES):
        total = total + values[:, start : start + LANES]
    return total


def as_row(column):
    return jnp.sum(jnp.transpose(column), axis=0, keepdims=True)


def as_column(row):
    return jnp.transpose(jnp.broadcast_to(row, (LANES, row.shape[1])))


def widen(column, width):
    return jnp.concatenate([column] * (width // LANES), axis=1)


def column_scale(valid, sums):
    keep = lax.broadcasted_iota(jnp.int32, sums.shape, 1) < valid
    return as_column(jnp.where(keep, 1.0 / sums, 0.0))


def tiles(ref, width, step):
    count = ref.shape[-1] // width

    def one(index, _):
        step(index // count, pl.ds(pl.multiple_of(lax.rem(index, count) * width, width), width))
        return 0

    lax.fori_loop(0, 2 * count, one, 0)


def copies(source_of, target_of, sems, count):
    return [pltpu.make_async_copy(source_of(at), target_of(at), sems.at[at]) for at in range(count)]


def first_kernel(
    valid, width, feats_ref, proj_ref, proto_ref, soft_ref, half_ref, col_ref, denom_ref, proto_half_ref,
    turned_ref, split_ref, raw_ref, acc_ref, unit_ref, in_ref, out_ref, raw_out_ref, in_sems, out_sems, raw_sems,
):
    count = half_ref.shape[-1] // width
    spans = [pl.ds(at * width, width) for at in range(count)]
    loads = copies(lambda at: feats_ref.at[spans[at]], lambda at: in_ref.at[spans[at]], in_sems, count)
    stores = copies(lambda at: out_ref.at[:, spans[at]], lambda at: split_ref.at[:, spans[at]], out_sems, count)
    raw_stores = copies(
        lambda at: raw_out_ref.at[:, :, spans[at]], lambda at: raw_ref.at[:, :, spans[at]], raw_sems, count
    )
    for load in loads:
        load.start()

    edge = valid // 8 * 8
    unit_ref[edge:] = jnp.zeros_like(unit_ref[edge:])
    unit_ref[:valid] = proto_ref[...]
    unit, _ = unit_rows(unit_ref[...])
    proto_half_ref[...] = unit.astype(jnp.bfloat16)
    turned_ref[...] = jnp.transpose(unit).astype(jnp.bfloat16)
    acc_ref[...] = jnp.zeros_like(acc_ref)

    for at in range(count):
        lanes = spans[at]
        loads[at].wait()
        out_ref[:, lanes] = jnp.transpose(in_ref[lanes], (1, 0, 2))
        stores[at].start()
        for view in range(2):
            raw = product(proj_ref[...], out_ref[view, lanes], NT)
            raw_out_ref[view, :, lanes] = raw
            unit, _ = unit_columns(raw)
            half = unit.astype(jnp.bfloat16)
            half_ref[view, :, lanes] = half
            denom = jnp.zeros((8, width), jnp.float32)
            for start in range(0, proto_half_ref.shape[0], CHUNK):
                logits = product(proto_half_ref[start : start + CHUNK], half, NN)
                soft = jnp.exp2(logits * (LOG2_E / SOFTMAX_TEMPER))
                if start + CHUNK > edge:
                    place = lax.broadcasted_iota(jnp.int32, soft.shape, 0) + start
                    soft = jnp.where(place < valid, soft, 0.0)
                soft_ref[view, start : start + CHUNK, lanes] = soft
                denom = denom + jnp.sum(soft.reshape(-1, 8, width), axis=0)
                acc_ref[view, start : start + CHUNK] += lane_sums(soft * soft)
            denom_ref[view, :, lanes] = jnp.sum(denom, axis=0, keepdims=True)
        raw_stores[at].start()

    for view in range(2):
        col_ref[view] = as_row(acc_ref[view])
    for store in stores + raw_stores:
        store.wait()


def row_kernel(valid, width, soft_ref, sums_ref, row_ref, scale_ref):
    for view in range(2):
        scale_ref[view] = column_scale(valid, sums_ref[view])

    def step(view, lanes):
        total = jnp.zeros((8, width), jnp.float32)
        for start in range(0, soft_ref.shape[1], 8):
            soft = soft_ref[view, start : start + 8, lanes]
            total = total + soft * soft * widen(scale_ref[view, start : start + 8], width)
        row_ref[view, :, lanes] = jnp.sum(total, axis=0, keepdims=True)

    tiles(row_ref, width, step)


def col_kernel(width, soft_ref, sums_ref, col_ref, acc_ref):
    acc_ref[...] = jnp.zeros_like(acc_ref)

    def step(view, lanes):
        scale = jnp.broadcast_to(1.0 / sums_ref[view, :, lanes], (8, width))
        for start in range(0, soft_ref.shape[1], 8):
            soft = soft_ref[view, start : start + 8, lanes]
            acc_ref[view, start : start + 8] += lane_sums(soft * soft * scale)

    tiles(sums_ref, width, step)
    for view in range(2):
        col_ref[view] = as_row(acc_ref[view])


def grad_kernel(
    valid, width, factor, feats_ref, raw_ref, proto_ref, turned_ref, half_ref, denom_ref, row_ref, col_ref,
    proto_out, proj_out, loss_ref, scale_ref, grad_ref, turn_ref, in_ref, raw_in_ref, in_sems, raw_sems,
):
    count = half_ref.shape[-1] // width
    spans = [pl.ds(at * width, width) for at in range(count)]
    loads = copies(lambda at: feats_ref.at[:, spans[at]], lambda at: in_ref.at[:, spans[at]], in_sems, count)
    raw_loads = copies(
        lambda at: raw_ref.at[:, :, spans[at]], lambda at: raw_in_ref.at[:, :, spans[at]], raw_sems, count
    )
    for at in range(count):
        raw_loads[at].start()
        loads[at].start()
    for view in range(2):
        scale_ref[view] = column_scale(valid, col_ref[view])
    loss = jnp.zeros((8, width), jnp.float32)
    for at in range(count):
        lanes = spans[at]
        both = lambda ref: jnp.concatenate([ref[view, :, lanes] for view in range(2)], axis=1)
        halves = [half_ref[view, :, lanes] for view in range(2)]
        for start in range(0, proto_ref.shape[0], CHUNK):
            part = slice(start, start + CHUNK)
            logits = [product(proto_ref[part], halves[view], NN) for view in range(2)]
            softs = [jnp.exp2(logits[view] * (LOG2_E / SOFTMAX_TEMPER)) for view in range(2)]
            for view in range(2):
                other = 1 - view
                target = softs[other] * softs[other] * widen(scale_ref[other, part], width)
                target = target * (factor / row_ref[other, :, lanes])
                loss = loss + jnp.sum((logits[view] * target).reshape(-1, 8, width), axis=0)
                grad = softs[view] * (factor / denom_ref[view, :, lanes]) - target
                grad_ref[part, view * width : (view + 1) * width] = grad.astype(jnp.bfloat16)
        proto_part = product(grad_ref[...], jnp.concatenate(halves, axis=1), NT)
        grad_unit = product(turned_ref[...], grad_ref[...], NN)
        raw_loads[at].wait()
        unit, inverse = unit_columns(both(raw_in_ref))
        along = jnp.sum(unit * grad_unit, axis=0, keepdims=True)
        grad_raw = ((grad_unit - unit * along) * inverse).astype(jnp.bfloat16)
        loads[at].wait()
        feats = jnp.concatenate([in_ref[view, lanes] for view in range(2)], axis=0)
        proj_part = product(grad_raw, feats, NN)
        if at == 0:
            proto_out[...] = proto_part
            turn_ref[...] = proj_part
        else:
            proto_out[...] += proto_part
            turn_ref[...] += proj_part

    proj_out[...] = jnp.transpose(turn_ref[...])
    logs = jnp.log(denom_ref[0]) + jnp.log(denom_ref[1])
    loss = jnp.sum(loss, axis=0, keepdims=True) * (1.0 / (SOFTMAX_TEMPER * factor))
    loss_ref[...] = jnp.broadcast_to(
        jnp.sum(loss, axis=1, keepdims=True) - jnp.sum(logs, axis=1, keepdims=True) * (1.0 / lax.axis_size("mp")),
        loss_ref.shape,
    )


IN_VMEM = pl.BlockSpec(memory_space=pltpu.VMEM)
IN_HBM = pl.BlockSpec(memory_space=pltpu.HBM)


def call(kernel, name, out_shapes, scratch, work, *args, far_in=(), far_out=()):
    outs = [
        pltpu.HBM(shape, dtype) if at in far_out else jax.ShapeDtypeStruct(shape, dtype)
        for at, (shape, dtype) in enumerate(out_shapes)
    ]
    return pl.pallas_call(
        kernel,
        in_specs=[IN_HBM if at in far_in else IN_VMEM for at in range(len(args))],
        out_specs=[IN_HBM if at in far_out else IN_VMEM for at in range(len(outs))],
        out_shape=outs,
        scratch_shapes=scratch,
        compiler_params=pltpu.CompilerParams(vmem_limit_bytes=VMEM_LIMIT),
        cost_estimate=pl.CostEstimate(flops=work, bytes_accessed=2**20, transcendentals=0), name=name,
    )(*args)


def body(features, projection, prototypes):
    rows = features.shape[0]
    shards = lax.axis_size("dp")
    batch_row_count = rows * shards
    factor = LOSS_FACTOR / (2.0 * batch_row_count * SOFTMAX_TEMPER)
    valid, width = prototypes.shape
    block = -(-valid // LANES) * LANES
    single, half_type = jnp.float32, jnp.bfloat16

    tile = min(512, rows)
    count = rows // tile
    row_shape, col_shape = ((2, 1, rows), single), ((2, 1, block), single)
    column = pltpu.VMEM((2, block, LANES), single)
    split = (2, rows, features.shape[-1])
    work = 4 * rows * block * width
    turned_proj = projection.T
    sems = pltpu.SemaphoreType.DMA((count,))
    far = lambda array: pltpu.with_memory_space_constraint(array, pltpu.HBM)
    soft, half, col_part, soft_part, proto_half, turned, feats, raw = call(
        functools.partial(first_kernel, valid, tile), "first_totals",
        [
            ((2, block, rows), single), ((2, width, rows), half_type), col_shape, row_shape,
            ((block, width), half_type), ((width, block), half_type), (split, half_type), ((2, width, rows), single),
        ],
        [
            column, pltpu.VMEM((block, width), single), pltpu.VMEM(features.shape, half_type),
            pltpu.VMEM(split, half_type), pltpu.VMEM((2, width, rows), single), sems, sems, sems,
        ],
        work, far(features), turned_proj, prototypes, far_in=(0,), far_out=(6, 7),
    )
    row_call = functools.partial(
        call, functools.partial(row_kernel, valid, min(512, rows)), "row_totals", [row_shape], [column], work, soft
    )
    col_call = functools.partial(
        call, functools.partial(col_kernel, min(512, rows)), "column_totals", [col_shape], [column], work, soft
    )

    col_sums = sum_over(col_part, "dp", 1)
    both = sum_over(jnp.concatenate([row_call(col_sums)[0], soft_part]), "mp", 2)
    row_sums, denoms = both[:2], both[2:]
    for iteration in range(1, ITERS):
        col_sums = sum_over(col_call(row_sums)[0], "dp", 1)
        row_sums = sum_over(row_call(col_sums)[0], "mp", 2)

    proto_part, proj_part, loss = call(
        functools.partial(grad_kernel, valid, tile, factor), "gradients",
        [((block, width), single), (projection.shape, single), ((8, width), single)],
        [
            column, pltpu.VMEM((block, 2 * tile), half_type), pltpu.VMEM(projection.shape[::-1], single),
            pltpu.VMEM(split, half_type), pltpu.VMEM((2, width, rows), single), sems, sems,
        ],
        3 * work, far(feats), far(raw), proto_half, turned, half, denoms, row_sums, col_sums, far_in=(0, 1),
    )
    loss_rows = jnp.broadcast_to(loss[None], (shards,) + loss.shape)
    proj_part = jnp.concatenate([proj_part.reshape(shards, -1, width), loss_rows], axis=1)
    proj_sum = sum_over(scatter_sum(proj_part, "dp", 1), "mp", 2)
    loss_value = -proj_sum[-1, 0] / (2.0 * batch_row_count)
    proj_grad = gather_blocks(proj_sum[:-8], "dp", 1).reshape(projection.shape)

    proto_sum = scatter_sum(proto_part.reshape(shards, -1, width), "dp", 1)
    proto_grad = gather_blocks(proto_sum, "dp", 1).reshape(block, width)[:valid]
    proto_unit, proto_inverse = unit_rows(prototypes)
    along_proto = jnp.sum(proto_unit * proto_grad, axis=-1, keepdims=True)
    grad_protos = (proto_grad - proto_unit * along_proto) * proto_inverse
    return (grad_protos, proj_grad, loss_value)


def solution(mesh):
    return jax.shard_map(
        body,
        mesh=mesh,
        in_specs=(P("dp", None, None), P(), P("mp", None)),
        out_specs=(P("mp", None), P(), P()),
        check_vma=False,
    )
```

```python
import functools

import jax
import jax.numpy as jnp
from jax import lax
from jax.experimental import pallas as pl
from jax.experimental.pallas import tpu as pltpu
from jax.sharding import PartitionSpec as P

ITERS = 3
EPSILON_CODES = 0.05
SOFTMAX_TEMPER = 0.1
LOSS_FACTOR = 4096.0
TINY = 1e-06
LOG2_E = 1.4426950408889634
LANES = 128
CHUNK = 256
FINAL_TYPE = jnp.float32
VMEM_LIMIT = 20 * 1024 * 1024


def swap(values, axis, size, offset):
    return lax.ppermute(values, axis, [(i, i ^ offset) for i in range(size)])


def stages(size, first):
    bits = size.bit_length() - 1
    groups, done = [], 0
    while done < bits:
        width = min(first if not groups else 2, bits - done)
        groups.append((done, width))
        done += width
    return groups


def sum_over(values, axis, first):
    size = lax.axis_size(axis)
    for low, width in stages(size, first):
        parts = [swap(values, axis, size, k << low) for k in reversed(range(1, 1 << width))]
        values = functools.reduce(jnp.add, parts, values)
    return values


def scatter_sum(values, axis, first):
    size = lax.axis_size(axis)
    me = lax.axis_index(axis)
    block = values.shape[1:]
    values = values[None]
    for low, width in stages(size, first):
        ways = 1 << width
        rest = values.shape[1] // ways
        values = values.reshape((rest, ways) + block)
        mine = (me >> low) & (ways - 1)
        own = lax.dynamic_index_in_dim(values, mine, 1, keepdims=False)
        for k in reversed(range(1, ways)):
            out = lax.dynamic_index_in_dim(values, mine ^ k, 1, keepdims=False)
            own = own + swap(out, axis, size, k << low)
        values = own[None]
    return values.reshape(block)


def gather_blocks(values, axis, first):
    size = lax.axis_size(axis)
    me = lax.axis_index(axis)
    block = values.shape
    values = values[None]
    for low, width in reversed(stages(size, first)):
        ways = 1 << width
        mine = (me >> low) & (ways - 1)
        parts = {k: swap(values, axis, size, k << low) if k else values for k in reversed(range(ways))}
        out = jnp.zeros((values.shape[0], ways) + block, values.dtype)
        for k, part in parts.items():
            out = lax.dynamic_update_slice_in_dim(out, part[:, None], mine ^ k, 1)
        values = out.reshape((-1,) + block)
    return values


NN = (((1,), (0,)), ((), ()))
NT = (((1,), (1,)), ((), ()))


def product(left, right, dims):
    return lax.dot_general(left, right, dims, preferred_element_type=jnp.float32)


def unit_rows(values):
    inverse = lax.rsqrt(jnp.sum(values * values, axis=-1, keepdims=True) + TINY)
    return (values * inverse, inverse)


def unit_columns(values):
    inverse = lax.rsqrt(jnp.sum(values * values, axis=0, keepdims=True) + TINY)
    return (values * inverse, inverse)


def lane_sums(values):
    total = values[:, :LANES]
    for start in range(LANES, values.shape[1], LANES):
        total = total + values[:, start : start + LANES]
    return total


def as_row(column):
    return jnp.sum(jnp.transpose(column), axis=0, keepdims=True)


def as_column(row):
    return jnp.transpose(jnp.broadcast_to(row, (LANES, row.shape[1])))


def widen(column, width):
    return jnp.concatenate([column] * (width // LANES), axis=1)


def column_scale(valid, sums):
    keep = lax.broadcasted_iota(jnp.int32, sums.shape, 1) < valid
    return as_column(jnp.where(keep, 1.0 / sums, 0.0))


def tiles(ref, width, step):
    count = ref.shape[-1] // width

    def one(index, _):
        step(index // count, pl.ds(pl.multiple_of(lax.rem(index, count) * width, width), width))
        return 0

    lax.fori_loop(0, 2 * count, one, 0)


def copies(source_of, target_of, sems, count):
    return [pltpu.make_async_copy(source_of(at), target_of(at), sems.at[at]) for at in range(count)]


def first_kernel(
    valid, width, feats_ref, proj_ref, proto_ref, codes_ref, col_ref, denom_ref, proto_half_ref,
    turned_ref, split_ref, raw_ref, acc_ref, unit_ref, in_ref, out_ref, raw_out_ref, proto_in_ref, in_sems,
    out_sems, raw_sems, proto_sems,
):
    count = denom_ref.shape[-1] // width
    spans = [pl.ds(at * width, width) for at in range(count)]
    proto_load = pltpu.make_async_copy(proto_ref, proto_in_ref, proto_sems.at[0])
    proto_load.start()
    loads = copies(lambda at: feats_ref.at[spans[at]], lambda at: in_ref.at[spans[at]], in_sems, count)
    stores = copies(lambda at: out_ref.at[:, spans[at]], lambda at: split_ref.at[:, spans[at]], out_sems, count)
    raw_stores = copies(
        lambda at: raw_out_ref.at[:, :, spans[at]], lambda at: raw_ref.at[:, :, spans[at]], raw_sems, count
    )
    for load in loads:
        load.start()

    edge = valid // 8 * 8
    unit_ref[edge:] = jnp.zeros_like(unit_ref[edge:])
    proto_load.wait()
    unit_ref[:valid] = proto_in_ref[...]
    unit, _ = unit_rows(unit_ref[...])
    proto_half_ref[...] = unit.astype(jnp.bfloat16)
    turned_ref[...] = jnp.transpose(unit).astype(jnp.bfloat16)
    acc_ref[...] = jnp.zeros_like(acc_ref)

    for at in range(count):
        lanes = spans[at]
        loads[at].wait()
        out_ref[:, lanes] = jnp.transpose(in_ref[lanes], (1, 0, 2))
        stores[at].start()
        for view in range(2):
            raw = product(proj_ref[...], out_ref[view, lanes], NT)
            raw_out_ref[view, :, lanes] = raw
            unit, _ = unit_columns(raw)
            half = unit.astype(jnp.bfloat16)
            denom = jnp.zeros((8, width), jnp.float32)
            for start in range(0, proto_half_ref.shape[0], CHUNK):
                logits = product(proto_half_ref[start : start + CHUNK], half, NN)
                soft = jnp.exp2(logits * (LOG2_E / SOFTMAX_TEMPER))
                if start + CHUNK > edge:
                    place = lax.broadcasted_iota(jnp.int32, soft.shape, 0) + start
                    soft = jnp.where(place < valid, soft, 0.0)
                code = soft * soft
                codes_ref[view, start : start + CHUNK, lanes] = code
                denom = denom + jnp.sum(soft.reshape(-1, 8, width), axis=0)
                acc_ref[view, start : start + CHUNK] += lane_sums(code)
            denom_ref[view, :, lanes] = jnp.sum(denom, axis=0, keepdims=True)
        raw_stores[at].start()

    for view in range(2):
        col_ref[view] = as_row(acc_ref[view])
    for store in stores + raw_stores:
        store.wait()


def row_kernel(valid, width, codes_ref, sums_ref, row_ref, scale_ref):
    for view in range(2):
        scale_ref[view] = column_scale(valid, sums_ref[view])

    def step(view, lanes):
        total = jnp.zeros((8, width), jnp.float32)
        for start in range(0, codes_ref.shape[1], 8):
            code = codes_ref[view, start : start + 8, lanes]
            total = total + code * widen(scale_ref[view, start : start + 8], width)
        row_ref[view, :, lanes] = jnp.sum(total, axis=0, keepdims=True)

    tiles(row_ref, width, step)


def col_kernel(width, codes_ref, sums_ref, col_ref, acc_ref):
    acc_ref[...] = jnp.zeros_like(acc_ref)

    def step(view, lanes):
        scale = jnp.broadcast_to(1.0 / sums_ref[view, :, lanes], (8, width))
        for start in range(0, codes_ref.shape[1], 8):
            code = codes_ref[view, start : start + 8, lanes]
            acc_ref[view, start : start + 8] += lane_sums(code * scale)

    tiles(sums_ref, width, step)
    for view in range(2):
        col_ref[view] = as_row(acc_ref[view])


def grad_kernel(
    valid, width, factor, feats_ref, raw_ref, proto_ref, turned_ref, denom_ref, row_ref, col_ref,
    proto_out, proj_out, loss_ref, scale_ref, grad_ref, turn_ref, in_ref, raw_in_ref, in_sems, raw_sems,
):
    count = row_ref.shape[-1] // width
    spans = [pl.ds(at * width, width) for at in range(count)]
    loads = copies(lambda at: feats_ref.at[:, spans[at]], lambda at: in_ref.at[:, spans[at]], in_sems, count)
    raw_loads = copies(
        lambda at: raw_ref.at[:, :, spans[at]], lambda at: raw_in_ref.at[:, :, spans[at]], raw_sems, count
    )
    for at in range(count):
        raw_loads[at].start()
        loads[at].start()
    for view in range(2):
        scale_ref[view] = column_scale(valid, col_ref[view])
    sides = [slice(view * width, (view + 1) * width) for view in range(2)]
    loss = jnp.zeros((8, width), jnp.float32)
    for at in range(count):
        lanes = spans[at]
        raw_loads[at].wait()
        raw = jnp.concatenate([raw_in_ref[view, :, lanes] for view in range(2)], axis=1)
        unit, inverse = unit_columns(raw)
        halves = unit.astype(jnp.bfloat16)
        for start in range(0, proto_ref.shape[0], CHUNK):
            part = slice(start, start + CHUNK)
            logits = [product(proto_ref[part], halves[:, side], NN) for side in sides]
            softs = [jnp.exp2(logits[view] * (LOG2_E / SOFTMAX_TEMPER)) for view in range(2)]
            for view in range(2):
                other = 1 - view
                target = softs[other] * softs[other] * widen(scale_ref[other, part], width)
                target = target * (factor / row_ref[other, :, lanes])
                loss = loss + jnp.sum((logits[view] * target).reshape(-1, 8, width), axis=0)
                grad = softs[view] * (factor / denom_ref[view, :, lanes]) - target
                grad_ref[part, sides[view]] = grad.astype(jnp.bfloat16)
        proto_part = product(grad_ref[...], halves, NT)
        grad_unit = product(turned_ref[...], grad_ref[...], NN)
        unit, inverse = unit_columns(raw)
        along = jnp.sum(unit * grad_unit, axis=0, keepdims=True)
        grad_raw = ((grad_unit - unit * along) * inverse).astype(jnp.bfloat16)
        loads[at].wait()
        feats = jnp.concatenate([in_ref[view, lanes] for view in range(2)], axis=0)
        proj_part = product(grad_raw, feats, NN)
        if at == 0:
            proto_out[...] = proto_part
            turn_ref[...] = proj_part
        else:
            proto_out[...] += proto_part
            turn_ref[...] += proj_part

    proj_out[...] = jnp.transpose(turn_ref[...])
    logs = jnp.log(denom_ref[0]) + jnp.log(denom_ref[1])
    loss = jnp.sum(loss, axis=0, keepdims=True) * (1.0 / (SOFTMAX_TEMPER * factor))
    loss_ref[...] = jnp.broadcast_to(
        jnp.sum(loss, axis=1, keepdims=True) - jnp.sum(logs, axis=1, keepdims=True) * (1.0 / lax.axis_size("mp")),
        loss_ref.shape,
    )


IN_VMEM = pl.BlockSpec(memory_space=pltpu.VMEM)
IN_HBM = pl.BlockSpec(memory_space=pltpu.HBM)


def call(kernel, name, out_shapes, scratch, work, *args, far_in=(), far_out=()):
    outs = [
        pltpu.HBM(shape, dtype) if at in far_out else jax.ShapeDtypeStruct(shape, dtype)
        for at, (shape, dtype) in enumerate(out_shapes)
    ]
    return pl.pallas_call(
        kernel,
        in_specs=[IN_HBM if at in far_in else IN_VMEM for at in range(len(args))],
        out_specs=[IN_HBM if at in far_out else IN_VMEM for at in range(len(outs))],
        out_shape=outs,
        scratch_shapes=scratch,
        compiler_params=pltpu.CompilerParams(vmem_limit_bytes=VMEM_LIMIT),
        cost_estimate=pl.CostEstimate(flops=work, bytes_accessed=2**20, transcendentals=0), name=name,
    )(*args)


def body(features, projection, prototypes):
    rows = features.shape[0]
    shards = lax.axis_size("dp")
    batch_row_count = rows * shards
    factor = LOSS_FACTOR / (2.0 * batch_row_count * SOFTMAX_TEMPER)
    valid, width = prototypes.shape
    block = -(-valid // LANES) * LANES
    single, half_type = jnp.float32, jnp.bfloat16

    tile = min(512, rows)
    count = rows // tile
    row_shape, col_shape = ((2, 1, rows), single), ((2, 1, block), single)
    column = pltpu.VMEM((2, block, LANES), single)
    split = (2, rows, features.shape[-1])
    work = 4 * rows * block * width
    turned_proj = projection.T
    sems = pltpu.SemaphoreType.DMA((count,))
    far = lambda array: pltpu.with_memory_space_constraint(array, pltpu.HBM)
    codes, col_part, soft_part, proto_half, turned, feats, raw = call(
        functools.partial(first_kernel, valid, tile), "first_totals",
        [
            ((2, block, rows), single), col_shape, row_shape, ((block, width), half_type),
            ((width, block), half_type), (split, half_type), ((2, width, rows), single),
        ],
        [
            column, pltpu.VMEM((block, width), single), pltpu.VMEM(features.shape, half_type),
            pltpu.VMEM(split, half_type), pltpu.VMEM((2, width, rows), single),
            pltpu.VMEM(prototypes.shape, single), sems, sems, sems, pltpu.SemaphoreType.DMA((1,)),
        ],
        work, far(features), turned_proj, far(prototypes), far_in=(0, 2), far_out=(5, 6),
    )
    row_call = functools.partial(
        call, functools.partial(row_kernel, valid, min(512, rows)), "row_totals", [row_shape], [column], work, codes
    )
    col_call = functools.partial(
        call, functools.partial(col_kernel, min(512, rows)), "column_totals", [col_shape], [column], work, codes
    )

    col_sums = sum_over(col_part, "dp", 1)
    both = sum_over(jnp.concatenate([row_call(col_sums)[0], soft_part]), "mp", 2)
    row_sums, denoms = both[:2], both[2:]
    for iteration in range(1, ITERS):
        col_sums = sum_over(col_call(row_sums)[0], "dp", 1)
        row_sums = sum_over(row_call(col_sums)[0], "mp", 2)

    proto_part, proj_part, loss = call(
        functools.partial(grad_kernel, valid, tile, factor), "gradients",
        [((block, width), single), (projection.shape, single), ((8, width), single)],
        [
            column, pltpu.VMEM((block, 2 * tile), half_type), pltpu.VMEM(projection.shape[::-1], single),
            pltpu.VMEM(split, half_type), pltpu.VMEM((2, width, rows), single), sems, sems,
        ],
        3 * work, far(feats), far(raw), proto_half, turned, denoms, row_sums, col_sums, far_in=(0, 1),
    )
    loss_rows = jnp.broadcast_to(loss[None], (shards,) + loss.shape)
    proj_part = jnp.concatenate([proj_part.reshape(shards, -1, width), loss_rows], axis=1)
    proj_sum = sum_over(scatter_sum(proj_part, "dp", 1), "mp", 2)
    loss_value = -proj_sum[-1, 0] / (2.0 * batch_row_count)

    share = block // shards
    proto_grad = scatter_sum(proto_part.reshape(shards, share, width), "dp", 1)
    mine = lax.dynamic_slice_in_dim(
        jnp.pad(prototypes, ((0, block - valid), (0, 0))), lax.axis_index("dp") * share, share, 0
    )
    proto_unit, proto_inverse = unit_rows(mine)
    along_proto = jnp.sum(proto_unit * proto_grad, axis=-1, keepdims=True)
    grad_share = (proto_grad - proto_unit * along_proto) * proto_inverse

    both = jnp.concatenate([grad_share, proj_sum[:-8]]).astype(FINAL_TYPE)
    both = gather_blocks(both, "dp", 1).astype(single)
    grad_protos = both[:, :share].reshape(block, width)[:valid]
    return (grad_protos, both[:, share:].reshape(projection.shape), loss_value)


def solution(mesh):
    return jax.shard_map(
        body,
        mesh=mesh,
        in_specs=(P("dp", None, None), P(), P("mp", None)),
        out_specs=(P("mp", None), P(), P()),
        check_vma=False,
    )
```

```python
import functools

import jax
import jax.numpy as jnp
from jax import lax
from jax.experimental import pallas as pl
from jax.experimental.pallas import tpu as pltpu
from jax.sharding import PartitionSpec as P

ITERS = 3
EPSILON_CODES = 0.05
SOFTMAX_TEMPER = 0.1
LOSS_FACTOR = 4096.0
TINY = 1e-06
LOG2_E = 1.4426950408889634
LANES = 128
CHUNK = 256
WIDE = 1024
FINAL_TYPE = jnp.bfloat16
VMEM_LIMIT = 22 * 1024 * 1024


def swap(values, axis, size, offset):
    return lax.ppermute(values, axis, [(i, i ^ offset) for i in range(size)])


def stages(size, first):
    bits = size.bit_length() - 1
    groups, done = [], 0
    while done < bits:
        width = min(first if not groups else 2, bits - done)
        groups.append((done, width))
        done += width
    return groups


def sum_over(values, axis, first):
    size = lax.axis_size(axis)
    for low, width in stages(size, first):
        parts = [swap(values, axis, size, k << low) for k in reversed(range(1, 1 << width))]
        values = functools.reduce(jnp.add, parts, values)
    return values


def scatter_sums(arrays, axis, groups):
    size = lax.axis_size(axis)
    me = lax.axis_index(axis)
    for low, width in groups:
        ways = 1 << width
        mine = (me >> low) & (ways - 1)
        split = [values.reshape((values.shape[0] // ways, ways) + values.shape[1:]) for values in arrays]
        pick = lambda values, at: lax.dynamic_index_in_dim(values, at, 1, keepdims=False)
        outs = [[pick(values, mine ^ k) for k in reversed(range(1, ways))] for values in split]
        outs = lax.optimization_barrier(outs)
        arrays = []
        for values, sent in zip(split, outs):
            own = pick(values, mine)
            for k, out in zip(reversed(range(1, ways)), sent):
                own = own + swap(out, axis, size, k << low)
            arrays.append(own)
    return arrays


def gather_blocks(values, axis, first):
    size = lax.axis_size(axis)
    me = lax.axis_index(axis)
    block = values.shape
    values = values[None]
    for low, width in reversed(stages(size, first)[1:]):
        ways = 1 << width
        mine = (me >> low) & (ways - 1)
        parts = {k: swap(values, axis, size, k << low) if k else values for k in reversed(range(ways))}
        out = jnp.zeros((values.shape[0], ways) + block, values.dtype)
        for k, part in parts.items():
            out = lax.dynamic_update_slice_in_dim(out, part[:, None], mine ^ k, 1)
        values = out.reshape((-1,) + block)
    return values


NN = (((1,), (0,)), ((), ()))
NT = (((1,), (1,)), ((), ()))


def product(left, right, dims):
    return lax.dot_general(left, right, dims, preferred_element_type=jnp.float32)


def unit_rows(values):
    inverse = lax.rsqrt(jnp.sum(values * values, axis=-1, keepdims=True) + TINY)
    return (values * inverse, inverse)


def unit_columns(values):
    inverse = lax.rsqrt(jnp.sum(values * values, axis=0, keepdims=True) + TINY)
    return (values * inverse, inverse)


def lane_sums(values):
    total = values[:, :LANES]
    for start in range(LANES, values.shape[1], LANES):
        total = total + values[:, start : start + LANES]
    return total


def as_row(column):
    return jnp.sum(jnp.transpose(column), axis=0, keepdims=True)


def as_column(row):
    return jnp.transpose(jnp.broadcast_to(row, (LANES, row.shape[1])))


def widen(column, width):
    return jnp.concatenate([column] * (width // LANES), axis=1)


def column_scale(valid, sums):
    keep = lax.broadcasted_iota(jnp.int32, sums.shape, 1) < valid
    return as_column(jnp.where(keep, 1.0 / sums, 0.0))


def tiles(ref, width, step):
    count = ref.shape[-1] // width

    def one(index, _):
        step(index // count, pl.ds(pl.multiple_of(lax.rem(index, count) * width, width), width))
        return 0

    lax.fori_loop(0, 2 * count, one, 0)


def copies(source_of, target_of, sems, count):
    return [pltpu.make_async_copy(source_of(at), target_of(at), sems.at[at]) for at in range(count)]


def first_kernel(
    valid, width, wide, feats_ref, proj_ref, proto_ref, codes_ref, col_ref, denom_ref, proto_half_ref,
    turned_ref, split_ref, raw_ref, acc_ref, unit_ref, in_ref, out_ref, raw_out_ref, proto_in_ref, proj_in_ref, proj_turned_ref, half_ref, in_sems,
    out_sems, raw_sems, proto_sems,
):
    count = denom_ref.shape[-1] // width
    spans = [pl.ds(at * width, width) for at in range(count)]
    proj_load = pltpu.make_async_copy(proj_ref, proj_in_ref, proto_sems.at[0])
    proto_load = pltpu.make_async_copy(proto_ref, proto_in_ref, proto_sems.at[1])
    loads = copies(lambda at: feats_ref.at[spans[at]], lambda at: in_ref.at[spans[at]], in_sems, count)
    stores = copies(lambda at: out_ref.at[:, spans[at]], lambda at: split_ref.at[:, spans[at]], out_sems, count)
    raw_stores = copies(
        lambda at: raw_out_ref.at[:, :, spans[at]], lambda at: raw_ref.at[:, :, spans[at]], raw_sems, count
    )
    for load in [proto_load, proj_load] + loads:
        load.start()

    edge = valid // 8 * 8
    unit_ref[edge:] = jnp.zeros_like(unit_ref[edge:])
    proto_load.wait()
    unit_ref[:valid] = proto_in_ref[...]
    unit, _ = unit_rows(unit_ref[...])
    proto_half_ref[...] = unit.astype(jnp.bfloat16)
    turned_ref[...] = jnp.transpose(unit).astype(jnp.bfloat16)
    proj_load.wait()
    proj_turned_ref[...] = jnp.transpose(proj_in_ref[...].astype(jnp.float32)).astype(jnp.bfloat16)

    for at in range(count):
        lanes = spans[at]
        loads[at].wait()
        out_ref[:, lanes] = jnp.transpose(in_ref[lanes], (1, 0, 2))
        stores[at].start()
        for view in range(2):
            raw = product(proj_turned_ref[...], out_ref[view, lanes], NT)
            raw_out_ref[view, :, lanes] = raw
            unit, _ = unit_columns(raw)
            half_ref[view, :, lanes] = unit.astype(jnp.bfloat16)
        raw_stores[at].start()

    for view in range(2):
        for low in range(0, half_ref.shape[-1], wide):
            lanes = slice(low, low + wide)
            half = half_ref[view, :, lanes]
            denom = jnp.zeros((8, wide), jnp.float32)
            for start in range(0, proto_half_ref.shape[0], CHUNK):
                part = slice(start, start + CHUNK)
                logits = product(proto_half_ref[part], half, NN)
                soft = jnp.exp2(logits * (LOG2_E / SOFTMAX_TEMPER))
                if start + CHUNK > edge:
                    place = lax.broadcasted_iota(jnp.int32, soft.shape, 0) + start
                    soft = jnp.where(place < valid, soft, 0.0)
                code = soft * soft
                codes_ref[view, part, lanes] = code
                denom = denom + jnp.sum(soft.reshape(-1, 8, wide), axis=0)
                total = lane_sums(code)
                acc_ref[view, part] = total if low == 0 else acc_ref[view, part] + total
            denom_ref[view, :, lanes] = jnp.sum(denom, axis=0, keepdims=True)

    for view in range(2):
        col_ref[view] = as_row(acc_ref[view])
    for store in stores + raw_stores:
        store.wait()


def row_kernel(valid, width, codes_ref, sums_ref, row_ref, scale_ref):
    for view in range(2):
        scale_ref[view] = column_scale(valid, sums_ref[view])

    def step(view, lanes):
        total = jnp.zeros((8, width), jnp.float32)
        for start in range(0, codes_ref.shape[1], 8):
            code = codes_ref[view, start : start + 8, lanes]
            total = total + code * widen(scale_ref[view, start : start + 8], width)
        row_ref[view, :, lanes] = jnp.sum(total, axis=0, keepdims=True)

    tiles(row_ref, width, step)


def col_kernel(width, codes_ref, sums_ref, col_ref, acc_ref):
    acc_ref[...] = jnp.zeros_like(acc_ref)

    def step(view, lanes):
        scale = jnp.broadcast_to(1.0 / sums_ref[view, :, lanes], (8, width))
        for start in range(0, codes_ref.shape[1], 8):
            code = codes_ref[view, start : start + 8, lanes]
            acc_ref[view, start : start + 8] += lane_sums(code * scale)

    tiles(sums_ref, width, step)
    for view in range(2):
        col_ref[view] = as_row(acc_ref[view])


def grad_kernel(
    valid, width, factor, feats_ref, raw_ref, proto_ref, turned_ref, denom_ref, row_ref, col_ref,
    out_ref, scale_ref, grad_ref, turn_ref, proto_sum_ref, in_ref, raw_in_ref, in_sems, raw_sems,
):
    count = row_ref.shape[-1] // width
    spans = [pl.ds(at * width, width) for at in range(count)]
    loads = copies(lambda at: feats_ref.at[:, spans[at]], lambda at: in_ref.at[:, spans[at]], in_sems, count)
    raw_loads = copies(
        lambda at: raw_ref.at[:, :, spans[at]], lambda at: raw_in_ref.at[:, :, spans[at]], raw_sems, count
    )
    for at in range(count):
        raw_loads[at].start()
        loads[at].start()
    for view in range(2):
        scale_ref[view] = column_scale(valid, col_ref[view])
    sides = [slice(view * width, (view + 1) * width) for view in range(2)]
    loss = jnp.zeros((8, width), jnp.float32)
    for at in range(count):
        lanes = spans[at]
        raw_loads[at].wait()
        raw = jnp.concatenate([raw_in_ref[view, :, lanes] for view in range(2)], axis=1)
        unit, inverse = unit_columns(raw)
        halves = unit.astype(jnp.bfloat16)
        for start in range(0, proto_ref.shape[0], CHUNK):
            part = slice(start, start + CHUNK)
            logits = [product(proto_ref[part], halves[:, side], NN) for side in sides]
            softs = [jnp.exp2(logits[view] * (LOG2_E / SOFTMAX_TEMPER)) for view in range(2)]
            for view in range(2):
                other = 1 - view
                target = softs[other] * softs[other] * widen(scale_ref[other, part], width)
                target = target * (factor / row_ref[other, :, lanes])
                loss = loss + jnp.sum((logits[view] * target).reshape(-1, 8, width), axis=0)
                grad = softs[view] * (factor / denom_ref[view, :, lanes]) - target
                grad_ref[part, sides[view]] = grad.astype(jnp.bfloat16)
        proto_part = product(grad_ref[...], halves, NT)
        grad_unit = product(turned_ref[...], grad_ref[...], NN)
        unit, inverse = unit_columns(raw)
        along = jnp.sum(unit * grad_unit, axis=0, keepdims=True)
        grad_raw = ((grad_unit - unit * along) * inverse).astype(jnp.bfloat16)
        loads[at].wait()
        feats = jnp.concatenate([in_ref[view, lanes] for view in range(2)], axis=0)
        proj_part = product(grad_raw, feats, NN)
        if at == 0:
            proto_sum_ref[...] = proto_part
            turn_ref[...] = proj_part
        else:
            proto_sum_ref[...] += proto_part
            turn_ref[...] += proj_part

    logs = jnp.log(denom_ref[0]) + jnp.log(denom_ref[1])
    loss = jnp.sum(loss, axis=0, keepdims=True) * (1.0 / (SOFTMAX_TEMPER * factor))
    loss = jnp.sum(loss, axis=1, keepdims=True) - jnp.sum(logs, axis=1, keepdims=True) * (1.0 / lax.axis_size("mp"))
    proj = jnp.transpose(turn_ref[...])
    shards = out_ref.shape[0]
    share, proj_share = proto_sum_ref.shape[0] // shards, proj.shape[0] // shards
    for at in range(shards):
        out_ref[at, :share] = proto_sum_ref[at * share : (at + 1) * share]
        out_ref[at, share : share + proj_share] = proj[at * proj_share : (at + 1) * proj_share]
        out_ref[at, share + proj_share :] = jnp.broadcast_to(loss, (8, out_ref.shape[-1]))


def assemble_kernel(share, side_ref, own_ref, other_ref, proto_out, proj_out):
    first = side_ref[0] == 0
    pairs, size, _ = own_ref.shape
    for pair in range(pairs):
        own, other = own_ref[pair].astype(jnp.float32), other_ref[pair].astype(jnp.float32)
        for core, block in enumerate([jnp.where(first, own, other), jnp.where(first, other, own)]):
            for out, part in ((proto_out, block[:share]), (proj_out, block[share:])):
                at = (2 * pair + core) * part.shape[0]
                rows = min(part.shape[0], out.shape[0] - at)
                if rows > 0:
                    out[at : at + rows] = part[:rows]


IN_VMEM = pl.BlockSpec(memory_space=pltpu.VMEM)
IN_HBM = pl.BlockSpec(memory_space=pltpu.HBM)


def call(kernel, name, out_shapes, scratch, work, *args, far_in=(), far_out=()):
    outs = [
        (pltpu.HBM if at in far_out else pltpu.VMEM)(shape, dtype)
        for at, (shape, dtype) in enumerate(out_shapes)
    ]
    return pl.pallas_call(
        kernel,
        in_specs=[IN_HBM if at in far_in else IN_VMEM for at in range(len(args))],
        out_specs=[IN_HBM if at in far_out else IN_VMEM for at in range(len(outs))],
        out_shape=outs,
        scratch_shapes=scratch,
        compiler_params=pltpu.CompilerParams(vmem_limit_bytes=VMEM_LIMIT),
        cost_estimate=pl.CostEstimate(flops=work, bytes_accessed=2**20, transcendentals=0), name=name,
    )(*args)


def body(features, projection, prototypes):
    rows = features.shape[0]
    shards = lax.axis_size("dp")
    batch_row_count = rows * shards
    factor = LOSS_FACTOR / (2.0 * batch_row_count * SOFTMAX_TEMPER)
    valid, width = prototypes.shape
    block = -(-valid // LANES) * LANES
    single, half_type = jnp.float32, jnp.bfloat16

    tile = min(1024, rows)
    share = block // shards
    count = rows // tile
    row_shape, col_shape = ((2, 1, rows), single), ((2, 1, block), single)
    column = pltpu.VMEM((2, block, LANES), single)
    split = (2, rows, features.shape[-1])
    work = 4 * rows * block * width
    sems = pltpu.SemaphoreType.DMA((count,))
    far = lambda array: pltpu.with_memory_space_constraint(array, pltpu.HBM)
    codes, col_part, soft_part, proto_half, turned, feats, raw = call(
        functools.partial(first_kernel, valid, tile, min(WIDE, rows)), "first_totals",
        [
            ((2, block, rows), single), col_shape, row_shape, ((block, width), half_type),
            ((width, block), half_type), (split, half_type), ((2, width, rows), single),
        ],
        [
            column, pltpu.VMEM((block, width), single), pltpu.VMEM(features.shape, half_type),
            pltpu.VMEM(split, half_type), pltpu.VMEM((2, width, rows), single),
            pltpu.VMEM(prototypes.shape, single), pltpu.VMEM(projection.shape, half_type),
            pltpu.VMEM(projection.shape[::-1], half_type), pltpu.VMEM((2, width, rows), half_type),
            sems, sems, sems, pltpu.SemaphoreType.DMA((2,)),
        ],
        work, far(features), far(projection), far(prototypes), far_in=(0, 1, 2), far_out=(5, 6),
    )
    row_call = functools.partial(
        call, functools.partial(row_kernel, valid, min(512, rows)), "row_totals", [row_shape], [column], work, codes
    )
    col_call = functools.partial(
        call, functools.partial(col_kernel, min(512, rows)), "column_totals", [col_shape], [column], work, codes
    )

    col_sums = sum_over(col_part, "dp", 1)
    both = sum_over(jnp.concatenate([row_call(col_sums)[0], soft_part]), "mp", 2)
    row_sums, denoms = both[:2], both[2:]
    for iteration in range(1, ITERS):
        col_sums = sum_over(col_call(row_sums)[0], "dp", 1)
        row_sums = sum_over(row_call(col_sums)[0], "mp", 2)

    parts = call(
        functools.partial(grad_kernel, valid, 1024, factor), "gradients",
        [((shards, share + projection.shape[0] // shards + 8, width), single)],
        [
            column, pltpu.VMEM((block, 2 * tile), half_type), pltpu.VMEM(projection.shape[::-1], single),
            pltpu.VMEM((block, width), single), pltpu.VMEM(split, half_type), pltpu.VMEM((2, width, rows), single), sems, sems,
        ],
        3 * work, far(feats), far(raw), proto_half, turned, denoms, row_sums, col_sums, far_in=(0, 1),
    )[0]
    pair, *others = stages(shards, 1)
    parts = scatter_sums([parts[:, share:], parts[:, :share]], "dp", [pair] + others)
    proj_part, proto_grad = [values[0] for values in parts]
    proj_sum = sum_over(proj_part, "mp", 2)
    loss_value = -proj_sum[-1, 0] / (2.0 * batch_row_count)
    mine = lax.dynamic_slice_in_dim(
        jnp.pad(prototypes, ((0, block - valid), (0, 0))), lax.axis_index("dp") * share, share, 0
    )
    proto_unit, proto_inverse = unit_rows(mine)
    along_proto = jnp.sum(proto_unit * proto_grad, axis=-1, keepdims=True)
    grad_share = (proto_grad - proto_unit * along_proto) * proto_inverse

    blocks = jnp.concatenate([grad_share, proj_sum[:-8]]).astype(FINAL_TYPE)
    blocks = gather_blocks(blocks, "dp", 1)
    other = swap(blocks, "dp", shards, 1)
    side = (lax.axis_index("dp") & 1).astype(jnp.int32).reshape(1)
    grad_protos, proj_grad = pl.pallas_call(
        functools.partial(assemble_kernel, share), in_specs=[pl.BlockSpec(memory_space=pltpu.SMEM), IN_VMEM, IN_VMEM],
        out_specs=[IN_VMEM, IN_VMEM],
        out_shape=[pltpu.HBM(prototypes.shape, single), pltpu.HBM(projection.shape, single)],
        compiler_params=pltpu.CompilerParams(vmem_limit_bytes=VMEM_LIMIT), name="assemble",
    )(side, blocks, other)
    return (grad_protos, proj_grad, loss_value)


def solution(mesh):
    return jax.shard_map(
        body,
        mesh=mesh,
        in_specs=(P("dp", None, None), P(), P("mp", None)),
        out_specs=(P("mp", None), P(), P()),
        check_vma=False,
    )
```

```python
import functools

import jax
import jax.numpy as jnp
from jax import lax
from jax.experimental import pallas as pl
from jax.experimental.pallas import tpu as pltpu
from jax.sharding import PartitionSpec as P

ITERS = 3
EPSILON_CODES = 0.05
SOFTMAX_TEMPER = 0.1
LOSS_FACTOR = 4096.0
TINY = 1e-06
LOG2_E = 1.4426950408889634
LANES = 128
CHUNK = 256
WIDE = 1024
FINAL_TYPE = jnp.bfloat16
VMEM_LIMIT = 22 * 1024 * 1024


def swap(values, axis, size, offset):
    return lax.ppermute(values, axis, [(i, i ^ offset) for i in range(size)])


def stages(size, first):
    bits = size.bit_length() - 1
    groups, done = [], 0
    while done < bits:
        width = min(first if not groups else 2, bits - done)
        groups.append((done, width))
        done += width
    return groups


def sum_over(values, axis, first):
    size = lax.axis_size(axis)
    for low, width in stages(size, first):
        parts = [swap(values, axis, size, k << low) for k in reversed(range(1, 1 << width))]
        values = functools.reduce(jnp.add, parts, values)
    return values


def scatter_sums(arrays, axis, groups):
    size = lax.axis_size(axis)
    me = lax.axis_index(axis)
    for low, width in groups:
        ways = 1 << width
        mine = (me >> low) & (ways - 1)
        split = [values.reshape((values.shape[0] // ways, ways) + values.shape[1:]) for values in arrays]
        pick = lambda values, at: lax.dynamic_index_in_dim(values, at, 1, keepdims=False)
        outs = [[pick(values, mine ^ k) for k in reversed(range(1, ways))] for values in split]
        outs = lax.optimization_barrier(outs)
        arrays = []
        for values, sent in zip(split, outs):
            own = pick(values, mine)
            for k, out in zip(reversed(range(1, ways)), sent):
                own = own + swap(out, axis, size, k << low)
            arrays.append(own)
    return arrays


def gather_blocks(values, axis, first):
    size = lax.axis_size(axis)
    me = lax.axis_index(axis)
    block = values.shape
    values = values[None]
    for low, width in reversed(stages(size, first)[1:]):
        ways = 1 << width
        mine = (me >> low) & (ways - 1)
        parts = {k: swap(values, axis, size, k << low) if k else values for k in reversed(range(ways))}
        out = jnp.zeros((values.shape[0], ways) + block, values.dtype)
        for k, part in parts.items():
            out = lax.dynamic_update_slice_in_dim(out, part[:, None], mine ^ k, 1)
        values = out.reshape((-1,) + block)
    return values


NN = (((1,), (0,)), ((), ()))
NT = (((1,), (1,)), ((), ()))


def product(left, right, dims):
    return lax.dot_general(left, right, dims, preferred_element_type=jnp.float32)


def unit_rows(values):
    inverse = lax.rsqrt(jnp.sum(values * values, axis=-1, keepdims=True) + TINY)
    return (values * inverse, inverse)


def unit_columns(values):
    inverse = lax.rsqrt(jnp.sum(values * values, axis=0, keepdims=True) + TINY)
    return (values * inverse, inverse)


def lane_sums(values):
    parts = [values[:, start : start + LANES] for start in range(0, values.shape[1], LANES)]
    while len(parts) > 1:
        parts = [a + b for a, b in zip(parts[::2], parts[1::2])] + parts[len(parts) - len(parts) % 2 :]
    return parts[0]


def as_row(column):
    return jnp.sum(jnp.transpose(column), axis=0, keepdims=True)


def as_column(row):
    return jnp.transpose(jnp.broadcast_to(row, (LANES, row.shape[1])))


def widen(column, width):
    return jnp.concatenate([column] * (width // LANES), axis=1)


def column_scale(valid, sums):
    keep = lax.broadcasted_iota(jnp.int32, sums.shape, 1) < valid
    return as_column(jnp.where(keep, 1.0 / sums, 0.0))


def tiles(ref, width, step):
    count = ref.shape[-1] // width

    def one(index, _):
        step(index // count, pl.ds(pl.multiple_of(lax.rem(index, count) * width, width), width))
        return 0

    lax.fori_loop(0, 2 * count, one, 0)


def copies(source_of, target_of, sems, count):
    return [pltpu.make_async_copy(source_of(at), target_of(at), sems.at[at]) for at in range(count)]


def first_kernel(
    valid, width, wide, feats_ref, proj_ref, proto_ref, codes_ref, col_ref, denom_ref, proto_half_ref,
    turned_ref, split_ref, raw_ref, acc_ref, unit_ref, in_ref, out_ref, raw_out_ref, proto_in_ref, proj_in_ref, proj_turned_ref, half_ref, in_sems,
    out_sems, raw_sems, proto_sems,
):
    count = denom_ref.shape[-1] // width
    spans = [pl.ds(at * width, width) for at in range(count)]
    proj_load = pltpu.make_async_copy(proj_ref, proj_in_ref, proto_sems.at[0])
    proto_load = pltpu.make_async_copy(proto_ref, proto_in_ref, proto_sems.at[1])
    loads = copies(lambda at: feats_ref.at[spans[at]], lambda at: in_ref.at[spans[at]], in_sems, count)
    stores = copies(lambda at: out_ref.at[:, spans[at]], lambda at: split_ref.at[:, spans[at]], out_sems, count)
    raw_stores = copies(
        lambda at: raw_out_ref.at[:, :, spans[at]], lambda at: raw_ref.at[:, :, spans[at]], raw_sems, count
    )
    for load in [proto_load, proj_load] + loads:
        load.start()

    edge = valid // 8 * 8
    unit_ref[edge:] = jnp.zeros_like(unit_ref[edge:])
    proto_load.wait()
    unit_ref[:valid] = proto_in_ref[...]
    unit, _ = unit_rows(unit_ref[...])
    proto_half_ref[...] = unit.astype(jnp.bfloat16)
    turned_ref[...] = jnp.transpose(unit).astype(jnp.bfloat16)
    proj_load.wait()
    proj_turned_ref[...] = jnp.transpose(proj_in_ref[...].astype(jnp.float32)).astype(jnp.bfloat16)

    for at in range(count):
        lanes = spans[at]
        loads[at].wait()
        out_ref[:, lanes] = jnp.transpose(in_ref[lanes], (1, 0, 2))
        stores[at].start()
        for view in range(2):
            raw = product(proj_turned_ref[...], out_ref[view, lanes], NT)
            raw_out_ref[view, :, lanes] = raw
            unit, _ = unit_columns(raw)
            half_ref[view, :, lanes] = unit.astype(jnp.bfloat16)
        raw_stores[at].start()

    for view in range(2):
        for low in range(0, half_ref.shape[-1], wide):
            lanes = slice(low, low + wide)
            half = half_ref[view, :, lanes]
            denom = jnp.zeros((8, wide), jnp.float32)
            for start in range(0, proto_half_ref.shape[0], CHUNK):
                part = slice(start, start + CHUNK)
                logits = product(proto_half_ref[part], half, NN)
                soft = jnp.exp2(logits * (LOG2_E / SOFTMAX_TEMPER))
                if start + CHUNK > edge:
                    place = lax.broadcasted_iota(jnp.int32, soft.shape, 0) + start
                    soft = jnp.where(place < valid, soft, 0.0)
                code = soft * soft
                codes_ref[view, part, lanes] = code
                denom = denom + jnp.sum(soft.reshape(-1, 8, wide), axis=0)
                total = lane_sums(code)
                acc_ref[view, part] = total if low == 0 else acc_ref[view, part] + total
            denom_ref[view, :, lanes] = jnp.sum(denom, axis=0, keepdims=True)

    for view in range(2):
        col_ref[view] = as_row(acc_ref[view])
    for store in stores + raw_stores:
        store.wait()


def row_kernel(valid, width, codes_ref, sums_ref, row_ref, scale_ref):
    for view in range(2):
        scale_ref[view] = column_scale(valid, sums_ref[view])

    def step(view, lanes):
        total = jnp.zeros((8, width), jnp.float32)
        for start in range(0, codes_ref.shape[1], 8):
            code = codes_ref[view, start : start + 8, lanes]
            total = total + code * widen(scale_ref[view, start : start + 8], width)
        row_ref[view, :, lanes] = jnp.sum(total, axis=0, keepdims=True)

    for view in range(2):
        for low in range(0, row_ref.shape[-1], width):
            step(view, slice(low, low + width))


def col_kernel(codes_ref, sums_ref, col_ref, acc_ref):
    for view in range(2):
        scale = jnp.broadcast_to(1.0 / sums_ref[view], (8, sums_ref.shape[-1]))
        for start in range(0, codes_ref.shape[1], 8):
            acc_ref[view, start : start + 8] = lane_sums(codes_ref[view, start : start + 8] * scale)
        col_ref[view] = as_row(acc_ref[view])


def grad_kernel(
    valid, width, factor, feats_ref, raw_ref, proto_ref, turned_ref, denom_ref, row_ref, col_ref,
    out_ref, scale_ref, grad_ref, turn_ref, proto_sum_ref, in_ref, raw_in_ref, in_sems, raw_sems,
):
    count = row_ref.shape[-1] // width
    spans = [pl.ds(at * width, width) for at in range(count)]
    loads = copies(lambda at: feats_ref.at[:, spans[at]], lambda at: in_ref.at[:, spans[at]], in_sems, count)
    raw_loads = copies(
        lambda at: raw_ref.at[:, :, spans[at]], lambda at: raw_in_ref.at[:, :, spans[at]], raw_sems, count
    )
    for at in range(count):
        raw_loads[at].start()
        loads[at].start()
    for view in range(2):
        scale_ref[view] = column_scale(valid, col_ref[view])
    sides = [slice(view * width, (view + 1) * width) for view in range(2)]
    loss = jnp.zeros((8, width), jnp.float32)
    for at in range(count):
        lanes = spans[at]
        raw_loads[at].wait()
        raw = jnp.concatenate([raw_in_ref[view, :, lanes] for view in range(2)], axis=1)
        unit, inverse = unit_columns(raw)
        halves = unit.astype(jnp.bfloat16)
        for start in range(0, proto_ref.shape[0], CHUNK):
            part = slice(start, start + CHUNK)
            logits = [product(proto_ref[part], halves[:, side], NN) for side in sides]
            softs = [jnp.exp2(logits[view] * (LOG2_E / SOFTMAX_TEMPER)) for view in range(2)]
            for view in range(2):
                other = 1 - view
                target = softs[other] * softs[other] * widen(scale_ref[other, part], width)
                target = target * (factor / row_ref[other, :, lanes])
                loss = loss + jnp.sum((logits[view] * target).reshape(-1, 8, width), axis=0)
                grad = softs[view] * (factor / denom_ref[view, :, lanes]) - target
                grad_ref[part, sides[view]] = grad.astype(jnp.bfloat16)
        proto_part = product(grad_ref[...], halves, NT)
        grad_unit = product(turned_ref[...], grad_ref[...], NN)
        unit, inverse = unit_columns(raw)
        along = jnp.sum(unit * grad_unit, axis=0, keepdims=True)
        grad_raw = ((grad_unit - unit * along) * inverse).astype(jnp.bfloat16)
        loads[at].wait()
        feats = jnp.concatenate([in_ref[view, lanes] for view in range(2)], axis=0)
        proj_part = product(grad_raw, feats, NN)
        if at == 0:
            proto_sum_ref[...] = proto_part
            turn_ref[...] = proj_part
        else:
            proto_sum_ref[...] += proto_part
            turn_ref[...] += proj_part

    logs = jnp.log(denom_ref[0]) + jnp.log(denom_ref[1])
    loss = jnp.sum(loss, axis=0, keepdims=True) * (1.0 / (SOFTMAX_TEMPER * factor))
    loss = jnp.sum(loss, axis=1, keepdims=True) - jnp.sum(logs, axis=1, keepdims=True) * (1.0 / lax.axis_size("mp"))
    proj = jnp.transpose(turn_ref[...])
    shards = out_ref.shape[0]
    share, proj_share = proto_sum_ref.shape[0] // shards, proj.shape[0] // shards
    for at in range(shards):
        out_ref[at, :share] = proto_sum_ref[at * share : (at + 1) * share]
        out_ref[at, share : share + proj_share] = proj[at * proj_share : (at + 1) * proj_share]
        out_ref[at, share + proj_share :] = jnp.broadcast_to(loss, (8, out_ref.shape[-1]))


def assemble_kernel(share, side_ref, own_ref, other_ref, proto_out, proj_out):
    first = side_ref[0] == 0
    pairs, size, _ = own_ref.shape
    for pair in range(pairs):
        own, other = own_ref[pair].astype(jnp.float32), other_ref[pair].astype(jnp.float32)
        for core, block in enumerate([jnp.where(first, own, other), jnp.where(first, other, own)]):
            for out, part in ((proto_out, block[:share]), (proj_out, block[share:])):
                at = (2 * pair + core) * part.shape[0]
                rows = min(part.shape[0], out.shape[0] - at)
                if rows > 0:
                    out[at : at + rows] = part[:rows]


IN_VMEM = pl.BlockSpec(memory_space=pltpu.VMEM)
IN_HBM = pl.BlockSpec(memory_space=pltpu.HBM)


def call(kernel, name, out_shapes, scratch, work, *args, far_in=(), far_out=()):
    outs = [
        (pltpu.HBM if at in far_out else pltpu.VMEM)(shape, dtype)
        for at, (shape, dtype) in enumerate(out_shapes)
    ]
    return pl.pallas_call(
        kernel,
        in_specs=[IN_HBM if at in far_in else IN_VMEM for at in range(len(args))],
        out_specs=[IN_HBM if at in far_out else IN_VMEM for at in range(len(outs))],
        out_shape=outs,
        scratch_shapes=scratch,
        compiler_params=pltpu.CompilerParams(vmem_limit_bytes=VMEM_LIMIT),
        cost_estimate=pl.CostEstimate(flops=work, bytes_accessed=2**20, transcendentals=0), name=name,
    )(*args)


def body(features, projection, prototypes):
    rows = features.shape[0]
    shards = lax.axis_size("dp")
    batch_row_count = rows * shards
    factor = LOSS_FACTOR / (2.0 * batch_row_count * SOFTMAX_TEMPER)
    valid, width = prototypes.shape
    block = -(-valid // LANES) * LANES
    single, half_type = jnp.float32, jnp.bfloat16

    tile = min(1024, rows)
    share = block // shards
    count = rows // tile
    row_shape, col_shape = ((2, 1, rows), single), ((2, 1, block), single)
    column = pltpu.VMEM((2, block, LANES), single)
    split = (2, rows, features.shape[-1])
    work = 4 * rows * block * width
    sems = pltpu.SemaphoreType.DMA((count,))
    far = lambda array: pltpu.with_memory_space_constraint(array, pltpu.HBM)
    codes, col_part, soft_part, proto_half, turned, feats, raw = call(
        functools.partial(first_kernel, valid, tile, min(WIDE, rows)), "first_totals",
        [
            ((2, block, rows), single), col_shape, row_shape, ((block, width), half_type),
            ((width, block), half_type), (split, half_type), ((2, width, rows), single),
        ],
        [
            column, pltpu.VMEM((block, width), single), pltpu.VMEM(features.shape, half_type),
            pltpu.VMEM(split, half_type), pltpu.VMEM((2, width, rows), single),
            pltpu.VMEM(prototypes.shape, single), pltpu.VMEM(projection.shape, half_type),
            pltpu.VMEM(projection.shape[::-1], half_type), pltpu.VMEM((2, width, rows), half_type),
            sems, sems, sems, pltpu.SemaphoreType.DMA((2,)),
        ],
        work, far(features), far(projection), far(prototypes), far_in=(0, 1, 2), far_out=(5, 6),
    )
    row_call = functools.partial(
        call, functools.partial(row_kernel, valid, min(1024, rows)), "row_totals", [row_shape], [column], work, codes
    )
    col_call = functools.partial(
        call, col_kernel, "column_totals", [col_shape], [column], work, codes
    )

    col_sums = sum_over(col_part, "dp", 1)
    both = sum_over(jnp.concatenate([row_call(col_sums)[0], soft_part]), "mp", 2)
    row_sums, denoms = both[:2], both[2:]
    for iteration in range(1, ITERS):
        col_sums = sum_over(col_call(row_sums)[0], "dp", 1)
        row_sums = sum_over(row_call(col_sums)[0], "mp", 2)

    parts = call(
        functools.partial(grad_kernel, valid, 1024, factor), "gradients",
        [((shards, share + projection.shape[0] // shards + 8, width), single)],
        [
            column, pltpu.VMEM((block, 2 * tile), half_type), pltpu.VMEM(projection.shape[::-1], single),
            pltpu.VMEM((block, width), single), pltpu.VMEM(split, half_type), pltpu.VMEM((2, width, rows), single), sems, sems,
        ],
        3 * work, far(feats), far(raw), proto_half, turned, denoms, row_sums, col_sums, far_in=(0, 1),
    )[0]
    parts = scatter_sums([parts[:, share:], parts[:, :share]], "dp", stages(shards, 1))
    proj_part, proto_grad = [values[0] for values in parts]
    proj_sum = sum_over(proj_part, "mp", 2)
    loss_value = -proj_sum[-1, 0] / (2.0 * batch_row_count)
    mine = lax.dynamic_slice_in_dim(
        jnp.pad(prototypes, ((0, block - valid), (0, 0))), lax.axis_index("dp") * share, share, 0
    )
    proto_unit, proto_inverse = unit_rows(mine)
    along_proto = jnp.sum(proto_unit * proto_grad, axis=-1, keepdims=True)
    grad_share = (proto_grad - proto_unit * along_proto) * proto_inverse

    blocks = jnp.concatenate([grad_share, proj_sum[:-8]]).astype(FINAL_TYPE)
    blocks = gather_blocks(blocks, "dp", 1)
    other = swap(blocks, "dp", shards, 1)
    side = (lax.axis_index("dp") & 1).astype(jnp.int32).reshape(1)
    grad_protos, proj_grad = pl.pallas_call(
        functools.partial(assemble_kernel, share), in_specs=[pl.BlockSpec(memory_space=pltpu.SMEM), IN_VMEM, IN_VMEM],
        out_specs=[IN_VMEM, IN_VMEM],
        out_shape=[pltpu.HBM(prototypes.shape, single), pltpu.HBM(projection.shape, single)],
        compiler_params=pltpu.CompilerParams(vmem_limit_bytes=VMEM_LIMIT), name="assemble",
    )(side, blocks, other)
    return (grad_protos, proj_grad, loss_value)


def solution(mesh):
    return jax.shard_map(
        body,
        mesh=mesh,
        in_specs=(P("dp", None, None), P(), P("mp", None)),
        out_specs=(P("mp", None), P(), P()),
        check_vma=False,
    )
```

```python
import functools

import jax
import jax.numpy as jnp
from jax import lax
from jax.experimental import pallas as pl
from jax.experimental.pallas import tpu as pltpu
from jax.sharding import PartitionSpec as P

ITERS = 3
EPSILON_CODES = 0.05
SOFTMAX_TEMPER = 0.1
LOSS_FACTOR = 4096.0
TINY = 1e-06
LOG2_E = 1.4426950408889634
LANES = 128
CHUNK = 256
WIDE = 1024
FINAL_TYPE = jnp.float32
VMEM_LIMIT = 22 * 1024 * 1024


def swap(values, axis, size, offset):
    return lax.ppermute(values, axis, [(i, i ^ offset) for i in range(size)])


def stages(size, first):
    bits = size.bit_length() - 1
    groups, done = [], 0
    while done < bits:
        width = min(first if not groups else 2, bits - done)
        groups.append((done, width))
        done += width
    return groups


def sum_over(values, axis, first):
    size = lax.axis_size(axis)
    for low, width in stages(size, first):
        parts = [swap(values, axis, size, k << low) for k in reversed(range(1, 1 << width))]
        values = functools.reduce(jnp.add, parts, values)
    return values


def scatter_sums(arrays, axis, groups):
    size = lax.axis_size(axis)
    me = lax.axis_index(axis)
    for low, width in groups:
        ways = 1 << width
        mine = (me >> low) & (ways - 1)
        split = [values.reshape((values.shape[0] // ways, ways) + values.shape[1:]) for values in arrays]
        pick = lambda values, at: lax.dynamic_index_in_dim(values, at, 1, keepdims=False)
        outs = [[pick(values, mine ^ k) for k in reversed(range(1, ways))] for values in split]
        outs = lax.optimization_barrier(outs)
        arrays = []
        for values, sent in zip(split, outs):
            own = pick(values, mine)
            for k, out in zip(reversed(range(1, ways)), sent):
                own = own + swap(out, axis, size, k << low)
            arrays.append(own)
    return arrays


def gather_blocks(values, axis, first):
    size = lax.axis_size(axis)
    me = lax.axis_index(axis)
    block = values.shape
    values = values[None]
    for low, width in reversed(stages(size, first)[1:]):
        ways = 1 << width
        mine = (me >> low) & (ways - 1)
        parts = {k: swap(values, axis, size, k << low) if k else values for k in reversed(range(ways))}
        out = jnp.zeros((values.shape[0], ways) + block, values.dtype)
        for k, part in parts.items():
            out = lax.dynamic_update_slice_in_dim(out, part[:, None], mine ^ k, 1)
        values = out.reshape((-1,) + block)
    return values


NN = (((1,), (0,)), ((), ()))
NT = (((1,), (1,)), ((), ()))


def product(left, right, dims):
    return lax.dot_general(left, right, dims, preferred_element_type=jnp.float32)


def unit_rows(values):
    inverse = lax.rsqrt(jnp.sum(values * values, axis=-1, keepdims=True) + TINY)
    return (values * inverse, inverse)


def unit_columns(values):
    inverse = lax.rsqrt(jnp.sum(values * values, axis=0, keepdims=True) + TINY)
    return (values * inverse, inverse)


def lane_sums(values):
    parts = [values[:, start : start + LANES] for start in range(0, values.shape[1], LANES)]
    while len(parts) > 1:
        parts = [a + b for a, b in zip(parts[::2], parts[1::2])] + parts[len(parts) - len(parts) % 2 :]
    return parts[0]


def as_row(column):
    return jnp.sum(jnp.transpose(column), axis=0, keepdims=True)


def as_column(row):
    return jnp.transpose(jnp.broadcast_to(row, (LANES, row.shape[1])))


def widen(column, width):
    return jnp.concatenate([column] * (width // LANES), axis=1)


def column_scale(valid, sums):
    keep = lax.broadcasted_iota(jnp.int32, sums.shape, 1) < valid
    return as_column(jnp.where(keep, 1.0 / sums, 0.0))


def tiles(ref, width, step):
    count = ref.shape[-1] // width

    def one(index, _):
        step(index // count, pl.ds(pl.multiple_of(lax.rem(index, count) * width, width), width))
        return 0

    lax.fori_loop(0, 2 * count, one, 0)


def copies(source_of, target_of, sems, count):
    return [pltpu.make_async_copy(source_of(at), target_of(at), sems.at[at]) for at in range(count)]


def first_kernel(
    valid, width, wide, feats_ref, proj_ref, proto_ref, codes_ref, col_ref, denom_ref, proto_half_ref,
    turned_ref, split_ref, raw_ref, acc_ref, unit_ref, in_ref, out_ref, raw_out_ref, proto_in_ref, proj_in_ref, proj_turned_ref, half_ref, in_sems,
    out_sems, raw_sems, proto_sems,
):
    count = denom_ref.shape[-1] // width
    spans = [pl.ds(at * width, width) for at in range(count)]
    proj_load = pltpu.make_async_copy(proj_ref, proj_in_ref, proto_sems.at[0])
    proto_load = pltpu.make_async_copy(proto_ref, proto_in_ref, proto_sems.at[1])
    loads = copies(lambda at: feats_ref.at[spans[at]], lambda at: in_ref.at[spans[at]], in_sems, count)
    stores = copies(lambda at: out_ref.at[:, spans[at]], lambda at: split_ref.at[:, spans[at]], out_sems, count)
    raw_stores = copies(
        lambda at: raw_out_ref.at[:, :, spans[at]], lambda at: raw_ref.at[:, :, spans[at]], raw_sems, count
    )
    for load in [proto_load, proj_load] + loads:
        load.start()

    edge = valid // 8 * 8
    unit_ref[edge:] = jnp.zeros_like(unit_ref[edge:])
    proto_load.wait()
    unit_ref[:valid] = proto_in_ref[...]
    unit, _ = unit_rows(unit_ref[...])
    proto_half_ref[...] = unit.astype(jnp.bfloat16)
    turned_ref[...] = jnp.transpose(unit).astype(jnp.bfloat16)
    proj_load.wait()
    proj_turned_ref[...] = jnp.transpose(proj_in_ref[...].astype(jnp.float32)).astype(jnp.bfloat16)

    for at in range(count):
        lanes = spans[at]
        loads[at].wait()
        out_ref[:, lanes] = jnp.transpose(in_ref[lanes], (1, 0, 2))
        stores[at].start()
        for view in range(2):
            raw = product(proj_turned_ref[...], out_ref[view, lanes], NT)
            raw_out_ref[view, :, lanes] = raw
            unit, _ = unit_columns(raw)
            half_ref[view, :, lanes] = unit.astype(jnp.bfloat16)
        raw_stores[at].start()

    for view in range(2):
        for low in range(0, half_ref.shape[-1], wide):
            lanes = slice(low, low + wide)
            half = half_ref[view, :, lanes]
            denom = jnp.zeros((8, wide), jnp.float32)
            for start in range(0, proto_half_ref.shape[0], CHUNK):
                part = slice(start, start + CHUNK)
                logits = product(proto_half_ref[part], half, NN)
                soft = jnp.exp2(logits * (LOG2_E / SOFTMAX_TEMPER))
                if start + CHUNK > edge:
                    place = lax.broadcasted_iota(jnp.int32, soft.shape, 0) + start
                    soft = jnp.where(place < valid, soft, 0.0)
                code = soft * soft
                codes_ref[view, part, lanes] = code
                denom = denom + jnp.sum(soft.reshape(-1, 8, wide), axis=0)
                total = lane_sums(code)
                acc_ref[view, part] = total if low == 0 else acc_ref[view, part] + total
            denom_ref[view, :, lanes] = jnp.sum(denom, axis=0, keepdims=True)

    for view in range(2):
        col_ref[view] = as_row(acc_ref[view])
    for store in stores + raw_stores:
        store.wait()


def row_kernel(valid, width, codes_ref, sums_ref, row_ref, scale_ref):
    for view in range(2):
        scale_ref[view] = column_scale(valid, sums_ref[view])

    def step(view, lanes):
        total = jnp.zeros((8, width), jnp.float32)
        for start in range(0, codes_ref.shape[1], 8):
            code = codes_ref[view, start : start + 8, lanes]
            total = total + code * widen(scale_ref[view, start : start + 8], width)
        row_ref[view, :, lanes] = jnp.sum(total, axis=0, keepdims=True)

    for view in range(2):
        for low in range(0, row_ref.shape[-1], width):
            step(view, slice(low, low + width))


def col_kernel(codes_ref, sums_ref, col_ref, acc_ref):
    for view in range(2):
        scale = jnp.broadcast_to(1.0 / sums_ref[view], (8, sums_ref.shape[-1]))
        for start in range(0, codes_ref.shape[1], 8):
            acc_ref[view, start : start + 8] = lane_sums(codes_ref[view, start : start + 8] * scale)
        col_ref[view] = as_row(acc_ref[view])


def grad_kernel(
    valid, width, factor, feats_ref, raw_ref, proto_ref, turned_ref, denom_ref, row_ref, col_ref,
    out_ref, scale_ref, grad_ref, turn_ref, proto_sum_ref, in_ref, raw_in_ref, in_sems, raw_sems,
):
    count = row_ref.shape[-1] // width
    spans = [pl.ds(at * width, width) for at in range(count)]
    loads = copies(lambda at: feats_ref.at[:, spans[at]], lambda at: in_ref.at[:, spans[at]], in_sems, count)
    raw_loads = copies(
        lambda at: raw_ref.at[:, :, spans[at]], lambda at: raw_in_ref.at[:, :, spans[at]], raw_sems, count
    )
    for at in range(count):
        raw_loads[at].start()
        loads[at].start()
    for view in range(2):
        scale_ref[view] = column_scale(valid, col_ref[view])
    sides = [slice(view * width, (view + 1) * width) for view in range(2)]
    loss = jnp.zeros((8, width), jnp.float32)
    for at in range(count):
        lanes = spans[at]
        raw_loads[at].wait()
        raw = jnp.concatenate([raw_in_ref[view, :, lanes] for view in range(2)], axis=1)
        unit, inverse = unit_columns(raw)
        halves = unit.astype(jnp.bfloat16)
        for start in range(0, proto_ref.shape[0], CHUNK):
            part = slice(start, start + CHUNK)
            logits = [product(proto_ref[part], halves[:, side], NN) for side in sides]
            softs = [jnp.exp2(logits[view] * (LOG2_E / SOFTMAX_TEMPER)) for view in range(2)]
            for view in range(2):
                other = 1 - view
                target = softs[other] * softs[other] * widen(scale_ref[other, part], width)
                target = target * (factor / row_ref[other, :, lanes])
                loss = loss + jnp.sum((logits[view] * target).reshape(-1, 8, width), axis=0)
                grad = softs[view] * (factor / denom_ref[view, :, lanes]) - target
                grad_ref[part, sides[view]] = grad.astype(jnp.bfloat16)
        proto_part = product(grad_ref[...], halves, NT)
        grad_unit = product(turned_ref[...], grad_ref[...], NN)
        unit, inverse = unit_columns(raw)
        along = jnp.sum(unit * grad_unit, axis=0, keepdims=True)
        grad_raw = ((grad_unit - unit * along) * inverse).astype(jnp.bfloat16)
        loads[at].wait()
        feats = jnp.concatenate([in_ref[view, lanes] for view in range(2)], axis=0)
        proj_part = product(grad_raw, feats, NN)
        if at == 0:
            proto_sum_ref[...] = proto_part
            turn_ref[...] = proj_part
        else:
            proto_sum_ref[...] += proto_part
            turn_ref[...] += proj_part

    logs = jnp.log(denom_ref[0]) + jnp.log(denom_ref[1])
    loss = jnp.sum(loss, axis=0, keepdims=True) * (1.0 / (SOFTMAX_TEMPER * factor))
    loss = jnp.sum(loss, axis=1, keepdims=True) - jnp.sum(logs, axis=1, keepdims=True) * (1.0 / lax.axis_size("mp"))
    proj = jnp.transpose(turn_ref[...])
    shards = out_ref.shape[0]
    share, proj_share = proto_sum_ref.shape[0] // shards, proj.shape[0] // shards
    for at in range(shards):
        out_ref[at, :share] = proto_sum_ref[at * share : (at + 1) * share]
        out_ref[at, share : share + proj_share] = proj[at * proj_share : (at + 1) * proj_share]
        out_ref[at, share + proj_share :] = jnp.broadcast_to(loss, (8, out_ref.shape[-1]))


def assemble_kernel(share, side_ref, own_ref, other_ref, proto_out, proj_out):
    first = side_ref[0] == 0
    pairs, size, _ = own_ref.shape
    for pair in range(pairs):
        own, other = own_ref[pair].astype(jnp.float32), other_ref[pair].astype(jnp.float32)
        for core, block in enumerate([jnp.where(first, own, other), jnp.where(first, other, own)]):
            for out, part in ((proto_out, block[:share]), (proj_out, block[share:])):
                at = (2 * pair + core) * part.shape[0]
                rows = min(part.shape[0], out.shape[0] - at)
                if rows > 0:
                    out[at : at + rows] = part[:rows]


IN_VMEM = pl.BlockSpec(memory_space=pltpu.VMEM)
IN_HBM = pl.BlockSpec(memory_space=pltpu.HBM)


def call(kernel, name, out_shapes, scratch, work, *args, far_in=(), far_out=()):
    outs = [
        (pltpu.HBM if at in far_out else pltpu.VMEM)(shape, dtype)
        for at, (shape, dtype) in enumerate(out_shapes)
    ]
    return pl.pallas_call(
        kernel,
        in_specs=[IN_HBM if at in far_in else IN_VMEM for at in range(len(args))],
        out_specs=[IN_HBM if at in far_out else IN_VMEM for at in range(len(outs))],
        out_shape=outs,
        scratch_shapes=scratch,
        compiler_params=pltpu.CompilerParams(vmem_limit_bytes=VMEM_LIMIT),
        cost_estimate=pl.CostEstimate(flops=work, bytes_accessed=2**20, transcendentals=0), name=name,
    )(*args)


def body(features, projection, prototypes):
    rows = features.shape[0]
    shards = lax.axis_size("dp")
    batch_row_count = rows * shards
    factor = LOSS_FACTOR / (2.0 * batch_row_count * SOFTMAX_TEMPER)
    valid, width = prototypes.shape
    block = -(-valid // LANES) * LANES
    single, half_type = jnp.float32, jnp.bfloat16

    tile = min(1024, rows)
    share = block // shards
    count = rows // tile
    row_shape, col_shape = ((2, 1, rows), single), ((2, 1, block), single)
    column = pltpu.VMEM((2, block, LANES), single)
    split = (2, rows, features.shape[-1])
    work = 4 * rows * block * width
    sems = pltpu.SemaphoreType.DMA((count,))
    far = lambda array: pltpu.with_memory_space_constraint(array, pltpu.HBM)
    codes, col_part, soft_part, proto_half, turned, feats, raw = call(
        functools.partial(first_kernel, valid, tile, min(WIDE, rows)), "first_totals",
        [
            ((2, block, rows), single), col_shape, row_shape, ((block, width), half_type),
            ((width, block), half_type), (split, half_type), ((2, width, rows), single),
        ],
        [
            column, pltpu.VMEM((block, width), single), pltpu.VMEM(features.shape, half_type),
            pltpu.VMEM(split, half_type), pltpu.VMEM((2, width, rows), single),
            pltpu.VMEM(prototypes.shape, single), pltpu.VMEM(projection.shape, half_type),
            pltpu.VMEM(projection.shape[::-1], half_type), pltpu.VMEM((2, width, rows), half_type),
            sems, sems, sems, pltpu.SemaphoreType.DMA((2,)),
        ],
        work, far(features), far(projection), far(prototypes), far_in=(0, 1, 2), far_out=(5, 6),
    )
    row_call = functools.partial(
        call, functools.partial(row_kernel, valid, min(1024, rows)), "row_totals", [row_shape], [column], work, codes
    )
    col_call = functools.partial(
        call, col_kernel, "column_totals", [col_shape], [column], work, codes
    )

    col_sums = sum_over(col_part, "dp", 1)
    both = sum_over(jnp.concatenate([row_call(col_sums)[0], soft_part]), "mp", 2)
    row_sums, denoms = both[:2], both[2:]
    for iteration in range(1, ITERS):
        col_sums = sum_over(col_call(row_sums)[0], "dp", 1)
        row_sums = sum_over(row_call(col_sums)[0], "mp", 2)

    parts = call(
        functools.partial(grad_kernel, valid, 1024, factor), "gradients",
        [((shards, share + projection.shape[0] // shards + 8, width), single)],
        [
            column, pltpu.VMEM((block, 2 * tile), half_type), pltpu.VMEM(projection.shape[::-1], single),
            pltpu.VMEM((block, width), single), pltpu.VMEM(split, half_type), pltpu.VMEM((2, width, rows), single), sems, sems,
        ],
        3 * work, far(feats), far(raw), proto_half, turned, denoms, row_sums, col_sums, far_in=(0, 1),
    )[0]
    parts = scatter_sums([parts[:, share:], parts[:, :share]], "dp", stages(shards, 1))
    proj_part, proto_grad = [values[0] for values in parts]
    proj_sum = sum_over(proj_part, "mp", 2)
    loss_value = -proj_sum[-1, 0] / (2.0 * batch_row_count)
    mine = lax.dynamic_slice_in_dim(
        jnp.pad(prototypes, ((0, block - valid), (0, 0))), lax.axis_index("dp") * share, share, 0
    )
    proto_unit, proto_inverse = unit_rows(mine)
    along_proto = jnp.sum(proto_unit * proto_grad, axis=-1, keepdims=True)
    grad_share = (proto_grad - proto_unit * along_proto) * proto_inverse

    blocks = jnp.concatenate([grad_share, proj_sum[:-8]]).astype(FINAL_TYPE)
    blocks = gather_blocks(blocks, "dp", 1)
    other = swap(blocks, "dp", shards, 1)
    side = (lax.axis_index("dp") & 1).astype(jnp.int32).reshape(1)
    grad_protos, proj_grad = pl.pallas_call(
        functools.partial(assemble_kernel, share), in_specs=[pl.BlockSpec(memory_space=pltpu.SMEM), IN_VMEM, IN_VMEM],
        out_specs=[IN_VMEM, IN_VMEM],
        out_shape=[pltpu.HBM(prototypes.shape, single), pltpu.HBM(projection.shape, single)],
        compiler_params=pltpu.CompilerParams(vmem_limit_bytes=VMEM_LIMIT), name="assemble",
    )(side, blocks, other)
    return (grad_protos, proj_grad, loss_value)


def solution(mesh):
    return jax.shard_map(
        body,
        mesh=mesh,
        in_specs=(P("dp", None, None), P(), P("mp", None)),
        out_specs=(P("mp", None), P(), P()),
        check_vma=False,
    )
```

```python
import functools

import jax
import jax.numpy as jnp
from jax import lax
from jax.experimental import pallas as pl
from jax.experimental.pallas import tpu as pltpu
from jax.sharding import PartitionSpec as P

ITERS = 3
EPSILON_CODES = 0.05
SOFTMAX_TEMPER = 0.1
LOSS_FACTOR = 4096.0
TINY = 1e-06
LOG2_E = 1.4426950408889634
LANES = 128
CHUNK = 256
GRAD_CHUNK = 384
WIDE = 1024
FINAL_TYPE = jnp.bfloat16
VMEM_LIMIT = 22 * 1024 * 1024


def swap(values, axis, size, offset):
    return lax.ppermute(values, axis, [(i, i ^ offset) for i in range(size)])


def stages(size, first):
    bits = size.bit_length() - 1
    groups, done = [], 0
    while done < bits:
        width = min(first if not groups else 2, bits - done)
        groups.append((done, width))
        done += width
    return groups


def sum_over(values, axis, first, wire=jnp.float32):
    size = lax.axis_size(axis)
    for low, width in stages(size, first):
        sent = values.astype(wire)
        order = (2, 3, 1) if width == 2 and axis == "mp" else reversed(range(1, 1 << width))
        parts = [swap(sent, axis, size, k << low).astype(values.dtype) for k in order]
        values = functools.reduce(jnp.add, parts, values)
    return values


def scatter_sums(arrays, axis, groups):
    size = lax.axis_size(axis)
    me = lax.axis_index(axis)
    for low, width in groups:
        ways = 1 << width
        mine = (me >> low) & (ways - 1)
        split = [values.reshape((values.shape[0] // ways, ways) + values.shape[1:]) for values in arrays]
        pick = lambda values, at: lax.dynamic_index_in_dim(values, at, 1, keepdims=False)
        outs = [[pick(values, mine ^ k) for k in reversed(range(1, ways))] for values in split]
        outs = lax.optimization_barrier(outs)
        arrays = []
        for values, sent in zip(split, outs):
            own = pick(values, mine)
            for k, out in zip(reversed(range(1, ways)), sent):
                own = own + swap(out, axis, size, k << low)
            arrays.append(own)
    return arrays


def gather_blocks(values, axis, first):
    size = lax.axis_size(axis)
    me = lax.axis_index(axis)
    block = values.shape
    values = values[None]
    for low, width in reversed(stages(size, first)[1:]):
        ways = 1 << width
        mine = (me >> low) & (ways - 1)
        parts = {k: swap(values, axis, size, k << low) if k else values for k in reversed(range(ways))}
        out = jnp.zeros((values.shape[0], ways) + block, values.dtype)
        for k, part in parts.items():
            out = lax.dynamic_update_slice_in_dim(out, part[:, None], mine ^ k, 1)
        values = out.reshape((-1,) + block)
    return values


NN = (((1,), (0,)), ((), ()))
NT = (((1,), (1,)), ((), ()))


def product(left, right, dims):
    return lax.dot_general(left, right, dims, preferred_element_type=jnp.float32)


def unit_rows(values):
    inverse = lax.rsqrt(jnp.sum(values * values, axis=-1, keepdims=True) + TINY)
    return (values * inverse, inverse)


def unit_columns(values):
    inverse = lax.rsqrt(jnp.sum(values * values, axis=0, keepdims=True) + TINY)
    return (values * inverse, inverse)


def lane_sums(values):
    parts = [values[:, start : start + LANES] for start in range(0, values.shape[1], LANES)]
    while len(parts) > 1:
        parts = [a + b for a, b in zip(parts[::2], parts[1::2])] + parts[len(parts) - len(parts) % 2 :]
    return parts[0]


def as_row(column):
    return jnp.sum(jnp.transpose(column), axis=0, keepdims=True)


def as_column(row):
    return jnp.transpose(jnp.broadcast_to(row, (LANES, row.shape[1])))


def widen(column, width):
    return jnp.concatenate([column] * (width // LANES), axis=1)


def column_scale(valid, sums):
    keep = lax.broadcasted_iota(jnp.int32, sums.shape, 1) < valid
    return as_column(jnp.where(keep, 1.0 / sums, 0.0))


def tiles(ref, width, step):
    count = ref.shape[-1] // width

    def one(index, _):
        step(index // count, pl.ds(pl.multiple_of(lax.rem(index, count) * width, width), width))
        return 0

    lax.fori_loop(0, 2 * count, one, 0)


def copies(source_of, target_of, sems, count):
    return [pltpu.make_async_copy(source_of(at), target_of(at), sems.at[at]) for at in range(count)]


def first_kernel(
    valid, width, wide, feats_ref, proj_ref, proto_ref, codes_ref, col_ref, denom_ref, proto_half_ref,
    turned_ref, split_ref, raw_ref, acc_ref, unit_ref, in_ref, out_ref, raw_out_ref, proto_in_ref, proj_in_ref, proj_turned_ref, half_ref, in_sems,
    out_sems, raw_sems, proto_sems,
):
    count = denom_ref.shape[-1] // width
    spans = [pl.ds(at * width, width) for at in range(count)]
    proj_load = pltpu.make_async_copy(proj_ref, proj_in_ref, proto_sems.at[0])
    proto_load = pltpu.make_async_copy(proto_ref, proto_in_ref, proto_sems.at[1])
    loads = copies(lambda at: feats_ref.at[spans[at]], lambda at: in_ref.at[spans[at]], in_sems, count)
    stores = copies(lambda at: out_ref.at[:, spans[at]], lambda at: split_ref.at[:, spans[at]], out_sems, count)
    raw_stores = copies(
        lambda at: raw_out_ref.at[:, :, spans[at]], lambda at: raw_ref.at[:, :, spans[at]], raw_sems, count
    )
    for load in [proto_load, proj_load] + loads:
        load.start()

    edge = valid // 8 * 8
    unit_ref[edge:] = jnp.zeros_like(unit_ref[edge:])
    proto_load.wait()
    unit_ref[:valid] = proto_in_ref[...]
    unit, _ = unit_rows(unit_ref[...])
    proto_half_ref[...] = unit.astype(jnp.bfloat16)
    turned_ref[...] = jnp.transpose(unit).astype(jnp.bfloat16)
    proj_load.wait()
    proj_turned_ref[...] = jnp.transpose(proj_in_ref[...].astype(jnp.float32)).astype(jnp.bfloat16)

    for at in range(count):
        lanes = spans[at]
        loads[at].wait()
        out_ref[:, lanes] = jnp.transpose(in_ref[lanes], (1, 0, 2))
        stores[at].start()
        for view in range(2):
            raw = product(proj_turned_ref[...], out_ref[view, lanes], NT)
            raw_out_ref[view, :, lanes] = raw
            unit, _ = unit_columns(raw)
            half_ref[view, :, lanes] = unit.astype(jnp.bfloat16)
        raw_stores[at].start()

    for view in range(2):
        for low in range(0, half_ref.shape[-1], wide):
            lanes = slice(low, low + wide)
            half = half_ref[view, :, lanes]
            denom = jnp.zeros((8, wide), jnp.float32)
            for start in range(0, proto_half_ref.shape[0], CHUNK):
                part = slice(start, start + CHUNK)
                logits = product(proto_half_ref[part], half, NN)
                soft = jnp.exp2(logits * (LOG2_E / SOFTMAX_TEMPER))
                if start + CHUNK > edge:
                    place = lax.broadcasted_iota(jnp.int32, soft.shape, 0) + start
                    soft = jnp.where(place < valid, soft, 0.0)
                code = soft * soft
                codes_ref[view, part, lanes] = code
                denom = denom + jnp.sum(soft.reshape(-1, 8, wide), axis=0)
                total = lane_sums(code)
                acc_ref[view, part] = total if low == 0 else acc_ref[view, part] + total
            denom_ref[view, :, lanes] = jnp.sum(denom, axis=0, keepdims=True)

    for view in range(2):
        col_ref[view] = as_row(acc_ref[view])
    for store in stores + raw_stores:
        store.wait()


def row_kernel(valid, width, codes_ref, sums_ref, row_ref, scale_ref):
    for view in range(2):
        scale_ref[view] = column_scale(valid, sums_ref[view])

    def step(view, lanes):
        total = jnp.zeros((8, width), jnp.float32)
        for start in range(0, codes_ref.shape[1], 8):
            code = codes_ref[view, start : start + 8, lanes]
            total = total + code * widen(scale_ref[view, start : start + 8], width)
        row_ref[view, :, lanes] = jnp.sum(total, axis=0, keepdims=True)

    for view in range(2):
        for low in range(0, row_ref.shape[-1], width):
            step(view, slice(low, low + width))


def col_kernel(codes_ref, sums_ref, col_ref, acc_ref):
    for view in range(2):
        scale = jnp.broadcast_to(1.0 / sums_ref[view], (8, sums_ref.shape[-1]))
        for start in range(0, codes_ref.shape[1], 8):
            acc_ref[view, start : start + 8] = lane_sums(codes_ref[view, start : start + 8] * scale)
        col_ref[view] = as_row(acc_ref[view])


def grad_kernel(
    valid, width, factor, feats_ref, raw_ref, proto_ref, turned_ref, denom_ref, row_ref, col_ref,
    out_ref, scale_ref, grad_ref, turn_ref, proto_sum_ref, in_ref, raw_in_ref, in_sems, raw_sems,
):
    count = row_ref.shape[-1] // width
    spans = [pl.ds(at * width, width) for at in range(count)]
    loads = copies(lambda at: feats_ref.at[:, spans[at]], lambda at: in_ref.at[:, spans[at]], in_sems, count)
    raw_loads = copies(
        lambda at: raw_ref.at[:, :, spans[at]], lambda at: raw_in_ref.at[:, :, spans[at]], raw_sems, count
    )
    for at in range(count):
        raw_loads[at].start()
        loads[at].start()
    for view in range(2):
        scale_ref[view] = column_scale(valid, col_ref[view])
    sides = [slice(view * width, (view + 1) * width) for view in range(2)]
    loss = jnp.zeros((8, width), jnp.float32)
    for at in range(count):
        lanes = spans[at]
        raw_loads[at].wait()
        raw = jnp.concatenate([raw_in_ref[view, :, lanes] for view in range(2)], axis=1)
        unit, inverse = unit_columns(raw)
        halves = unit.astype(jnp.bfloat16)
        row_scales = [factor / row_ref[view, :, lanes] for view in range(2)]
        denom_scales = [factor / denom_ref[view, :, lanes] for view in range(2)]
        for start in range(0, proto_ref.shape[0], GRAD_CHUNK):
            part = slice(start, start + GRAD_CHUNK)
            logits = [product(proto_ref[part], halves[:, side], NN) for side in sides]
            softs = [jnp.exp2(logits[view] * (LOG2_E / SOFTMAX_TEMPER)) for view in range(2)]
            for view in range(2):
                other = 1 - view
                target = softs[other] * softs[other] * widen(scale_ref[other, part], width)
                target = target * row_scales[other]
                loss = loss + jnp.sum((logits[view] * target).reshape(-1, 8, width), axis=0)
                grad = softs[view] * denom_scales[view] - target
                grad_ref[part, sides[view]] = grad.astype(jnp.bfloat16)
        proto_part = product(grad_ref[...], halves, NT)
        grad_unit = product(turned_ref[...], grad_ref[...], NN)
        unit, inverse = unit_columns(raw)
        along = jnp.sum(unit * grad_unit, axis=0, keepdims=True)
        grad_raw = ((grad_unit - unit * along) * inverse).astype(jnp.bfloat16)
        loads[at].wait()
        feats = jnp.concatenate([in_ref[view, lanes] for view in range(2)], axis=0)
        proj_part = product(grad_raw, feats, NN)
        if at == 0:
            proto_sum_ref[...] = proto_part
            turn_ref[...] = proj_part
        else:
            proto_sum_ref[...] += proto_part
            turn_ref[...] += proj_part

    logs = jnp.log(denom_ref[0]) + jnp.log(denom_ref[1])
    loss = jnp.sum(loss, axis=0, keepdims=True) * (1.0 / (SOFTMAX_TEMPER * factor))
    loss = jnp.sum(loss, axis=1, keepdims=True) - jnp.sum(logs, axis=1, keepdims=True) * (1.0 / lax.axis_size("mp"))
    proj = jnp.transpose(turn_ref[...])
    shards = out_ref.shape[0]
    share, proj_share = proto_sum_ref.shape[0] // shards, proj.shape[0] // shards
    for at in range(shards):
        out_ref[at, :share] = proto_sum_ref[at * share : (at + 1) * share]
        out_ref[at, share : share + proj_share] = proj[at * proj_share : (at + 1) * proj_share]
        out_ref[at, share + proj_share :] = jnp.broadcast_to(loss, (8, out_ref.shape[-1]))


def assemble_kernel(share, side_ref, own_ref, other_ref, proto_out, proj_out):
    first = side_ref[0] == 0
    pairs, size, _ = own_ref.shape
    for pair in range(pairs):
        own, other = own_ref[pair].astype(jnp.float32), other_ref[pair].astype(jnp.float32)
        for core, block in enumerate([jnp.where(first, own, other), jnp.where(first, other, own)]):
            for out, part in ((proto_out, block[:share]), (proj_out, block[share:])):
                at = (2 * pair + core) * part.shape[0]
                rows = min(part.shape[0], out.shape[0] - at)
                if rows > 0:
                    out[at : at + rows] = part[:rows]


IN_VMEM = pl.BlockSpec(memory_space=pltpu.VMEM)
IN_HBM = pl.BlockSpec(memory_space=pltpu.HBM)


def call(kernel, name, out_shapes, scratch, work, *args, far_in=(), far_out=()):
    outs = [
        (pltpu.HBM if at in far_out else pltpu.VMEM)(shape, dtype)
        for at, (shape, dtype) in enumerate(out_shapes)
    ]
    return pl.pallas_call(
        kernel,
        in_specs=[IN_HBM if at in far_in else IN_VMEM for at in range(len(args))],
        out_specs=[IN_HBM if at in far_out else IN_VMEM for at in range(len(outs))],
        out_shape=outs,
        scratch_shapes=scratch,
        compiler_params=pltpu.CompilerParams(vmem_limit_bytes=VMEM_LIMIT),
        cost_estimate=pl.CostEstimate(flops=work, bytes_accessed=2**20, transcendentals=0), name=name,
    )(*args)


def body(features, projection, prototypes):
    rows = features.shape[0]
    shards = lax.axis_size("dp")
    batch_row_count = rows * shards
    factor = LOSS_FACTOR / (2.0 * batch_row_count * SOFTMAX_TEMPER)
    valid, width = prototypes.shape
    block = -(-valid // LANES) * LANES
    single, half_type = jnp.float32, jnp.bfloat16

    tile = min(1024, rows)
    share = block // shards
    count = rows // tile
    row_shape, col_shape = ((2, 1, rows), single), ((2, 1, block), single)
    column = pltpu.VMEM((2, block, LANES), single)
    split = (2, rows, features.shape[-1])
    work = 4 * rows * block * width
    sems = pltpu.SemaphoreType.DMA((count,))
    far = lambda array: pltpu.with_memory_space_constraint(array, pltpu.HBM)
    codes, col_part, soft_part, proto_half, turned, feats, raw = call(
        functools.partial(first_kernel, valid, tile, min(WIDE, rows)), "first_totals",
        [
            ((2, block, rows), single), col_shape, row_shape, ((block, width), half_type),
            ((width, block), half_type), (split, half_type), ((2, width, rows), single),
        ],
        [
            column, pltpu.VMEM((block, width), single), pltpu.VMEM(features.shape, half_type),
            pltpu.VMEM(split, half_type), pltpu.VMEM((2, width, rows), single),
            pltpu.VMEM(prototypes.shape, single), pltpu.VMEM(projection.shape, half_type),
            pltpu.VMEM(projection.shape[::-1], half_type), pltpu.VMEM((2, width, rows), half_type),
            sems, sems, sems, pltpu.SemaphoreType.DMA((2,)),
        ],
        work, far(features), far(projection), far(prototypes), far_in=(0, 1, 2), far_out=(5, 6),
    )
    row_call = functools.partial(
        call, functools.partial(row_kernel, valid, min(1024, rows)), "row_totals", [row_shape], [column], work, codes
    )
    col_call = functools.partial(
        call, col_kernel, "column_totals", [col_shape], [column], work, codes
    )

    col_sums = sum_over(col_part, "dp", 1)
    both = sum_over(jnp.concatenate([row_call(col_sums)[0], soft_part]), "mp", 2)
    row_sums, denoms = both[:2], both[2:]
    for iteration in range(1, ITERS):
        col_sums = sum_over(col_call(row_sums)[0], "dp", 1)
        wire = single if iteration == ITERS - 1 else half_type
        row_sums = sum_over(row_call(col_sums)[0], "mp", 2, wire)

    parts = call(
        functools.partial(grad_kernel, valid, 1024, factor), "gradients",
        [((shards, share + projection.shape[0] // shards + 8, width), single)],
        [
            column, pltpu.VMEM((block, 2 * tile), half_type), pltpu.VMEM(projection.shape[::-1], single),
            pltpu.VMEM((block, width), single), pltpu.VMEM(split, half_type), pltpu.VMEM((2, width, rows), single), sems, sems,
        ],
        3 * work, far(feats), far(raw), proto_half, turned, denoms, row_sums, col_sums, far_in=(0, 1),
    )[0]
    parts = scatter_sums([parts[:, share:], parts[:, :share]], "dp", stages(shards, 1))
    proj_part, proto_grad = [values[0] for values in parts]
    proj_sum = sum_over(proj_part, "mp", 2)
    loss_value = -proj_sum[-1, 0] / (2.0 * batch_row_count)
    mine = lax.dynamic_slice_in_dim(
        jnp.pad(prototypes, ((0, block - valid), (0, 0))), lax.axis_index("dp") * share, share, 0
    )
    proto_unit, proto_inverse = unit_rows(mine)
    along_proto = jnp.sum(proto_unit * proto_grad, axis=-1, keepdims=True)
    grad_share = (proto_grad - proto_unit * along_proto) * proto_inverse

    blocks = jnp.concatenate([grad_share, proj_sum[:-8]]).astype(FINAL_TYPE)
    blocks = gather_blocks(blocks, "dp", 1)
    other = swap(blocks, "dp", shards, 1)
    side = (lax.axis_index("dp") & 1).astype(jnp.int32).reshape(1)
    grad_protos, proj_grad = pl.pallas_call(
        functools.partial(assemble_kernel, share), in_specs=[pl.BlockSpec(memory_space=pltpu.SMEM), IN_VMEM, IN_VMEM],
        out_specs=[IN_VMEM, IN_VMEM],
        out_shape=[pltpu.HBM(prototypes.shape, single), pltpu.HBM(projection.shape, single)],
        compiler_params=pltpu.CompilerParams(vmem_limit_bytes=VMEM_LIMIT), name="assemble",
    )(side, blocks, other)
    return (grad_protos, proj_grad, loss_value)


def solution(mesh):
    return jax.shard_map(
        body,
        mesh=mesh,
        in_specs=(P("dp", None, None), P(), P("mp", None)),
        out_specs=(P("mp", None), P(), P()),
        check_vma=False,
    )
```
